128 devices in a mesh: row: 8 (over y, core), col: 16 (over x, z).
Axes of the slice: x: 4, y: 4, z: 4, core: 2. Of those that a mesh axis runs over, the one named last changes fastest.
Arguments:
- tokens: bfloat16 [1024, 18432], P(None, ('row', 'col')), may hold values from -200 to 200
- layer_norm_gain: bfloat16 [18432], P(('row', 'col')), may hold values from 0.099609375 to 1.8984375
- query_weight: bfloat16 [18432, 12288], P('row', 'col'), may hold values from -0.046875 to 0.046875
- kv_weight: bfloat16 [18432, 512], P('row'), may hold values from -0.046875 to 0.046875
- output_weight_matrix: bfloat16 [12288, 18432], P('col', 'row'), may hold values from -0.5 to 0.5
- kv_cache: bfloat16 [1024, 2048, 512], P(('row', 'col')), may hold values from -1000 to 1000
- lengths: int32 [1024], P(('row', 'col')), may hold values from 2 to 2048, as said below
Outputs:
- branch: bfloat16 [1024, 18432], P(None, ('row', 'col'))
- new_kv: bfloat16 [1024, 512], P(('row', 'col'))
The draws below stay inside these ranges and needn't reach their ends.
Inputs may be any that keep to these rules, and one draw needn't show every extreme that they name: `lengths`: some row has exactly 2048 valid positions and some row exactly 2.
All inputs are finite; a program needn't handle non-finite values.
Results may differ from the reference program's by a relative error of at most 0.02.
Values may be sent and summed in bfloat16 or wider, within the bound.
A program may use at most 128 MiB of HBM per device.

```python
import math
import jax
import jax.numpy as jnp
from jax import lax

D = 18432
HEADS = 48
HD = 256
CACHE = 2048
ROWS_DEV = 8
HQ = 12288
ROWS = 1024


def cache_lengths(key):
    key = jax.random.fold_in(key, 41)
    first, second, third, fourth, fifth = jax.random.split(key, 5)
    groups = ROWS // ROWS_DEV
    scale_factors = jax.random.randint(first, (3, ROWS), 0, 64, jnp.int32)
    product = scale_factors[0] * scale_factors[1] * scale_factors[2]
    short_rows = 2 + product * (CACHE - 2) // 250047
    long_rows = CACHE - jax.random.randint(second, (ROWS,), 0, CACHE // 16 + 1, jnp.int32)
    order = jax.random.permutation(third, groups)
    device_long = order < (groups + 1) // 2
    row_long = jnp.repeat(device_long, ROWS_DEV)
    result = jnp.where(row_long, long_rows, short_rows)
    longest = jax.random.randint(fourth, (), 0, ROWS, jnp.int32)
    shortest_row = (longest + 1 + jax.random.randint(fifth, (), 0, ROWS - 1, jnp.int32)) % ROWS
    result = result.at[longest].set(CACHE)
    result = result.at[shortest_row].set(2)
    return result.astype(jnp.int32)


def draw_tokens(key, part):
    key = jax.random.fold_in(key, 11)
    first, second = jax.random.split(key, 2)
    column_scale = 0.3 * 10.0 ** (jnp.arange(D, dtype=jnp.float32) / D)
    row_scale = jnp.exp(jax.random.uniform(second, (ROWS, 1), jnp.float32, 0.0, math.log(10.0)))
    base = jax.random.normal(first, (ROWS, D), jnp.float32)
    base = jnp.clip(base, -6.0, 6.0)
    return (base * column_scale[None, :] * row_scale).astype(jnp.bfloat16)


def draw_kv_cache(key, part):
    key = jax.random.fold_in(key, 23)
    first = jax.random.fold_in(key, 0)
    shape = (ROWS, CACHE, 2 * HD)
    cache = jnp.clip(jax.random.normal(first, shape, jnp.float32), -6.0, 6.0)
    return cache.astype(jnp.bfloat16)


def draw_lengths(key, part):
    return cache_lengths(key)


def levels(stream_key, shape, cuts, smallest, largest):
    loudness, own = 1.0, jax.random.fold_in(stream_key, 6)
    for dim, shards_of in cuts:
        steps = jnp.exp(jax.random.uniform(jax.random.fold_in(own, dim), (shards_of,), jnp.float32, smallest / len(cuts), largest / len(cuts)))
        loudness = loudness * jnp.repeat(steps, shape[dim] // shards_of).reshape([-1 if axis == dim else 1 for axis in range(len(shape))])
    return loudness


def scatter_about(rng, extent, deviation, bound, cuts=(), kind=jnp.bfloat16):
    factor_of = levels(rng, extent, cuts, -0.22, 0.18) if cuts else 1.0
    array = jax.random.normal(rng, extent, jnp.float32) * deviation * factor_of
    return jnp.minimum(jnp.maximum(array, -bound), bound).astype(kind)


def setup_inputs(seed: int = 0) -> dict:
    splits = jax.random.split(jax.random.key(seed), 8)
    return {
        "tokens": draw_tokens(jax.random.fold_in(splits[7], 71), 0),
        "layer_norm_gain": jnp.clip(1.0 + 0.18 * jax.random.normal(splits[1], (D,), jnp.float32), 0.099609375, 1.8984375).astype(jnp.bfloat16),
        "query_weight": scatter_about(splits[2], (D, HQ), D ** -0.5, 0.046875, ((0, 8), (1, 16))),
        "kv_weight": scatter_about(splits[3], (D, 2 * HD), D ** -0.5, 0.046875, ((0, 8),)),
        "output_weight_matrix": scatter_about(splits[4], (HQ, D), (HD // 2) ** -0.5, 0.5, ((0, 16), (1, 8))),
        "kv_cache": draw_kv_cache(jax.random.fold_in(splits[7], 71), 0),
        "lengths": draw_lengths(jax.random.fold_in(splits[7], 71), 0),
    }


EPSILON = 1e-05
NEGATIVE_FLOOR = -1e+30

def normalize(value_rows, gain, total_sum, total_sq, width):
    floats = value_rows.astype(jnp.float32)
    average = total_sum / width
    inverse = lax.rsqrt(total_sq / width - average * average + EPSILON)
    return (floats - average[:, None]) * inverse[:, None] * gain.astype(jnp.float32)[None, :]

def row_attention(inputs):
    queries, cache, fresh, length = inputs
    score_scale = HD ** (-0.5)
    query_float = queries.astype(jnp.float32)
    keys = cache[:, :HD].astype(jnp.float32)
    value_rows = cache[:, HD:].astype(jnp.float32)
    scores = jnp.einsum('hd,kd->hk', query_float, keys) * score_scale
    valid = jnp.arange(CACHE, dtype=jnp.int32)[None, :] < length
    scores = jnp.where(valid, scores, NEGATIVE_FLOOR)
    new_scores = jnp.einsum('hd,d->h', query_float, fresh[:HD].astype(jnp.float32)) * score_scale
    highest = jnp.maximum(lax.optimization_barrier(jnp.max(scores, axis=1)), new_scores)
    attention_probabilities = jnp.where(valid, jnp.exp(scores - highest[:, None]), 0.0)
    new_probs = jnp.exp(new_scores - highest)
    weight_sum = lax.optimization_barrier(jnp.sum(attention_probabilities, axis=1)) + new_probs
    rounded = attention_probabilities.astype(jnp.bfloat16).astype(jnp.float32)
    context = jnp.einsum('hk,kd->hd', rounded, value_rows)
    context = context + new_probs.astype(jnp.bfloat16).astype(jnp.float32)[:, None] * fresh[HD:].astype(jnp.float32)[None, :]
    return (context / weight_sum[:, None]).astype(jnp.bfloat16)

def reference(tokens, layer_norm_gain, query_weight, kv_weight, output_weight_matrix, kv_cache, lengths):
    floats = tokens.astype(jnp.float32)
    normed = normalize(tokens, layer_norm_gain, lax.optimization_barrier(jnp.sum(floats, axis=1)), lax.optimization_barrier(jnp.sum(floats * floats, axis=1)), D).astype(jnp.bfloat16)
    queries = jnp.dot(normed, query_weight, preferred_element_type=jnp.float32).astype(jnp.bfloat16)
    new_kv = jnp.dot(normed, kv_weight, preferred_element_type=jnp.float32).astype(jnp.bfloat16)
    context = lax.map(row_attention, (queries.reshape(ROWS, HEADS, HD), kv_cache, new_kv, lengths))
    context = context.reshape(ROWS, HQ)
    branch = jnp.dot(context, output_weight_matrix, preferred_element_type=jnp.float32).astype(jnp.bfloat16)
    return (branch, new_kv)
```

```python
import functools

import jax
import jax.numpy as jnp
from jax import lax
from jax.experimental import pallas as pl
from jax.experimental.pallas import tpu as pltpu
from jax.sharding import PartitionSpec as P

MESH = pl.DeviceIdType.MESH
EPSILON = 1e-05
NEGATIVE_FLOOR = -1e30
HD = 256
SIDE = 4
VMEM_BYTES = 56 * 1024 * 1024


def rcopy(src, dst, send_sem, recv_sem, device):
    return pltpu.make_async_remote_copy(
        src_ref=src,
        dst_ref=dst,
        send_sem=send_sem,
        recv_sem=recv_sem,
        device_id=device,
        device_id_type=MESH,
    )


def along(ax, x, z, step):
    if ax == 0:
        return ((x + step + SIDE) % SIDE) * SIDE + z
    return x * SIDE + (z + step + SIDE) % SIDE


def loop(low, high, body):
    def step(i, carry):
        body(i)
        return carry

    lax.fori_loop(low, high, step, 0)


def greet(peers):
    barrier = pltpu.get_barrier_semaphore()
    count = 0
    for number, device_of in peers:

        def hello(d, device_of=device_of):
            pl.semaphore_signal(barrier, inc=1, device_id=device_of(d), device_id_type=MESH)

        loop(0, number, hello)
        count += number
    pl.semaphore_wait(barrier, count)


def project_kernel(
    n_features,
    tok,
    gain,
    wq,
    wkv,
    q_out,
    kv_out,
    xbuf,
    wbuf,
    gexp,
    xn,
    part,
    psend,
    own,
    qs,
    qrecv,
    stx,
    stz,
    sty,
    stc,
    smsg,
    zmsg,
    ymsg,
    cmsg,
    mi,
    w_sem,
    gs,
    gr,
    ps,
    pr,
    qsem,
    qrsem,
    sts,
    str_,
):
    r, c = lax.axis_index("row"), lax.axis_index("col")
    x, z = c // SIDE, c % SIDE
    y, core = r // 2, r % 2
    chunks, feats, lanes = tok.shape
    half = 80
    head_cols = wq.shape[1]
    n_col = SIDE * SIDE

    load_q = pltpu.make_async_copy(wq, wbuf.at[:, pl.ds(0, head_cols)], w_sem.at[0])
    load_kv = pltpu.make_async_copy(
        wkv.at[:, pl.ds(pl.multiple_of(x * 128, 128), 128)],
        wbuf.at[:, pl.ds(head_cols, 128)],
        w_sem.at[1],
    )
    load_q.start()
    load_kv.start()

    sums, squares = [], []
    for k in range(chunks):
        t = tok[k].astype(jnp.float32)
        sums.append(jnp.sum(t, axis=0, keepdims=True))
        squares.append(jnp.sum(t * t, axis=0, keepdims=True))
    smsg[0:8] = jnp.concatenate(sums, axis=0)
    smsg[8:16] = jnp.concatenate(squares, axis=0)
    smsg[16:24] = gain[...]
    stx[x] = smsg[...]

    def keep(j):
        xbuf[j, x, z] = tok[(r + 1 + j) % chunks]

    loop(0, chunks, keep)

    greet(
        [
            (n_col - 1, lambda d: (r, (c + 1 + d) % n_col)),
            (chunks - 1, lambda d: ((r + 1 + d) % chunks, c)),
        ]
    )

    def stat_x(d):
        return rcopy(smsg, stx.at[x], sts.at[d], str_.at[d], (r, along(0, x, z, d + 1)))

    def stat_z(d):
        return rcopy(zmsg, stz.at[z], sts.at[3 + d], str_.at[3 + d], (r, along(1, x, z, d + 1)))

    def stat_y(d):
        return rcopy(ymsg, sty.at[y], sts.at[6 + d], str_.at[6 + d], ((r + 2 * d + 2) % 8, c))

    stat_c = rcopy(cmsg, stc.at[core], sts.at[9], str_.at[9], (r + 1 - 2 * core, c))

    loop(0, 3, lambda d: stat_x(d).start())

    def block(ax, j, i):
        return xbuf.at[j, (i + SIDE) % SIDE, z] if ax == 0 else xbuf.at[j, x, (i + SIDE) % SIDE]

    def rows_of(ref, si):
        return ref.at[pl.ds(0, half)] if si == 0 else ref.at[pl.ds(half, feats - half)]

    def group(ax, j, i, low, n):
        i = (i + SIDE) % SIDE
        return xbuf.at[j, pl.ds(low, n), i] if ax == 0 else xbuf.at[j, i, pl.ds(low, n)]

    def first(ax, j, si):
        s = 1 - 2 * si
        here = block(ax, j, x if ax == 0 else z)
        return rcopy(here, here, gs.at[j, si], gr.at[j, si], (r, along(ax, x, z, s)))

    def first_on(ax, j, si):
        s = 1 - 2 * si
        ref = rows_of(block(ax, j, (x if ax == 0 else z) - s), si)
        return rcopy(ref, ref, gs.at[j, 2 + si], gr.at[j, 2 + si], (r, along(ax, x, z, s)))

    def second(ax, j, si):
        s = 1 - 2 * si
        ref = group(ax, j, z if ax == 0 else x, 0, SIDE)
        return rcopy(ref, ref, gs.at[j, 4 + si], gr.at[j, 4 + si], (r, along(1 - ax, x, z, s)))

    def second_on(ax, j, si):
        s = 1 - 2 * si
        ref = group(ax, j, (z if ax == 0 else x) - s, 2 * si, 2)
        return rcopy(ref, ref, gs.at[j, 6 + si], gr.at[j, 6 + si], (r, along(1 - ax, x, z, s)))

    def both(p, do):
        for si in (0, 1):
            for ax in (0, 1):
                do(ax, 2 * p + ax, si)

    pairs = chunks // 2
    loop(0, pairs, lambda p: both(p, lambda ax, j, si: first(ax, j, si).start()))

    loop(0, 3, lambda d: stat_x(d).wait_recv())
    zmsg[0:16] = stx[0, 0:16] + stx[1, 0:16] + stx[2, 0:16] + stx[3, 0:16]
    for i in range(SIDE):
        zmsg[16 + 8 * i : 24 + 8 * i] = stx[i, 16:24]
    stz[z] = zmsg[...]
    loop(0, 3, lambda d: stat_z(d).start())

    def forward(p):
        def do(ax, j, si):
            first(ax, j, si).wait_recv()
            first_on(ax, j, si).start()

        both(p, do)

    loop(0, pairs, forward)

    def start_second(p):
        both(p, lambda ax, j, si: first_on(ax, j, si).wait_recv())
        both(p, lambda ax, j, si: second(ax, j, si).start())

    loop(0, 2, start_second)

    loop(0, 3, lambda d: stat_z(d).wait_recv())
    ymsg[...] = stz[0, 0:16] + stz[1, 0:16] + stz[2, 0:16] + stz[3, 0:16]
    sty[y] = ymsg[...]
    loop(0, 3, lambda d: stat_y(d).start())

    def spread(i):
        rows = stz[i % SIDE, pl.ds(pl.multiple_of(16 + 8 * (i // SIDE), 8), 8)]
        gexp[i, 0:128] = jnp.broadcast_to(rows[0:1], (128, 128)).T
        gexp[i, 128:feats] = jnp.broadcast_to(rows[1:2], (128, 128)).T[0 : feats - 128]

    loop(0, n_col, spread)

    loop(0, 3, lambda d: stat_y(d).wait_recv())
    cmsg[...] = sty[0] + sty[1] + sty[2] + sty[3]
    stc[core] = cmsg[...]
    stat_c.start()
    stat_c.wait_recv()
    total = stc[0] + stc[1]
    average = total[0:8] / n_features
    mi[0:8] = average
    mi[8:16] = lax.rsqrt(total[8:16] / n_features - average * average + EPSILON)

    load_q.wait()
    load_kv.wait()

    def partial_send(j):
        return rcopy(psend.at[j], part.at[j], ps.at[j], pr.at[j], ((r + 1 + j) % chunks, c))

    def compute(j):
        k = (r + 1 + j) % chunks
        mean, inverse = mi[pl.ds(k, 1), :], mi[pl.ds(8 + k, 1), :]
        for i in range(n_col):
            t = xbuf[j, i // SIDE, i % SIDE].astype(jnp.float32)
            xn[feats * i : feats * (i + 1)] = ((t - mean) * inverse * gexp[i]).astype(jnp.bfloat16)
        return lax.dot_general(
            xn[...], wbuf[...], (((0,), (0,)), ((), ())), preferred_element_type=jnp.float32
        )

    def pair(p):
        @pl.when(p < pairs - 2)
        def _():
            start_second(p + 2)

        def do(ax, j, si):
            second(ax, j, si).wait_recv()
            second_on(ax, j, si).start()

        both(p, do)
        both(p, lambda ax, j, si: second_on(ax, j, si).wait_recv())

        def one(i):
            j = 2 * p + i
            own[...] = compute(j)

            @pl.when(j < chunks - 1)
            def _():
                psend[j] = own[...].astype(jnp.bfloat16)
                partial_send(j).start()

        loop(0, 2, one)

    loop(0, pairs, pair)

    loop(0, chunks - 1, lambda j: partial_send(j).wait_recv())
    acc = own[...]
    for j in range(chunks - 1):
        acc = acc + part[j].astype(jnp.float32)
    for i in range(qs.shape[0]):
        qs[i] = acc[:, 128 * i : 128 * (i + 1)]

    rows_dev = q_out.shape[0]

    def row_send(d):
        to = (c + 1 + d) % n_col
        return rcopy(
            qs.at[:, pl.ds(pl.multiple_of(to * rows_dev, 8), rows_dev)],
            qrecv.at[:, pl.ds(pl.multiple_of(c * rows_dev, 8), rows_dev)],
            qsem.at[d],
            qrsem.at[d],
            (r, to),
        )

    loop(0, n_col - 1, lambda d: row_send(d).start())
    mine = pl.ds(pl.multiple_of(c * rows_dev, 8), rows_dev)
    qrecv[:, mine] = qs[:, mine]
    loop(0, n_col - 1, lambda d: row_send(d).wait_recv())
    for b in range(rows_dev):
        for i in range(head_cols // 128):
            at = slice(n_col * (i // 2), n_col * (i // 2 + 1))
            q_out[b, at, 128 * (i % 2) : 128 * (i % 2 + 1)] = qrecv[
                i, pl.ds(b, n_col, stride=rows_dev)
            ].astype(jnp.bfloat16)
    for i in range(SIDE):
        kv_out[:, 128 * i : 128 * (i + 1)] = qrecv[
            head_cols // 128, 8 * SIDE * i : 8 * SIDE * i + 8
        ].astype(jnp.bfloat16)

    loop(0, 3, lambda d: stat_x(d).wait_send())
    loop(0, 3, lambda d: stat_z(d).wait_send())
    loop(0, 3, lambda d: stat_y(d).wait_send())
    stat_c.wait_send()

    def sent(p):
        for send in (first, first_on, second, second_on):
            both(p, lambda ax, j, si: send(ax, j, si).wait_send())

    loop(0, pairs, sent)
    loop(0, chunks - 1, lambda j: partial_send(j).wait_send())
    loop(0, n_col - 1, lambda d: row_send(d).wait_send())


def project(tokens, gain, query_weight, kv_weight, n_features, heads, rows_dev):
    chunks, feats, lanes = tokens.shape
    depth, head_cols = query_weight.shape
    wide = head_cols + 128
    n_col = SIDE * SIDE
    f32, bf16 = jnp.float32, jnp.bfloat16
    vmem = pl.BlockSpec(memory_space=pltpu.VMEM)
    anywhere = pl.BlockSpec(memory_space=pl.ANY)
    dma = pltpu.SemaphoreType.DMA
    return pl.pallas_call(
        functools.partial(project_kernel, n_features),
        out_shape=(
            jax.ShapeDtypeStruct((rows_dev, heads, HD), bf16),
            jax.ShapeDtypeStruct((rows_dev, kv_weight.shape[1]), bf16),
        ),
        in_specs=[vmem, vmem, anywhere, anywhere],
        out_specs=(vmem, vmem),
        scratch_shapes=[
            pltpu.VMEM((chunks, SIDE, SIDE, feats, lanes), bf16),
            pltpu.VMEM((depth, wide), bf16),
            pltpu.VMEM((n_col, feats, lanes), f32),
            pltpu.VMEM((depth, lanes), bf16),
            pltpu.VMEM((chunks - 1, lanes, wide), bf16),
            pltpu.VMEM((chunks - 1, lanes, wide), bf16),
            pltpu.VMEM((lanes, wide), f32),
            pltpu.VMEM((wide // 128, lanes, 128), f32),
            pltpu.VMEM((wide // 128, lanes, 128), f32),
            pltpu.VMEM((SIDE, 24, lanes), f32),
            pltpu.VMEM((SIDE, 48, lanes), f32),
            pltpu.VMEM((SIDE, 16, lanes), f32),
            pltpu.VMEM((2, 16, lanes), f32),
            pltpu.VMEM((24, lanes), f32),
            pltpu.VMEM((48, lanes), f32),
            pltpu.VMEM((16, lanes), f32),
            pltpu.VMEM((16, lanes), f32),
            pltpu.VMEM((16, lanes), f32),
            dma((2,)),
            dma((chunks, 8)),
            dma((chunks, 8)),
            dma((chunks - 1,)),
            dma((chunks - 1,)),
            dma((n_col - 1,)),
            dma((n_col - 1,)),
            dma((10,)),
            dma((10,)),
        ],
        compiler_params=pltpu.CompilerParams(
            collective_id=0, has_side_effects=True, vmem_limit_bytes=VMEM_BYTES
        ),
        name="project",
    )(tokens, gain, query_weight, kv_weight)


def attend_kernel(lengths, q_ref, kv_ref, cache, out):
    b = pl.program_id(0)
    rows_dev = pl.num_programs(0)
    positions = cache.shape[1]
    scale = HD**-0.5
    q = q_ref[0]
    fresh = kv_ref[pl.ds(b, 1), :]
    new_key, new_value = fresh[:, :HD], fresh[:, HD:]
    scores = (
        lax.dot_general(
            q, cache[0, :, :HD], (((1,), (1,)), ((), ())), preferred_element_type=jnp.float32
        )
        * scale
    )
    position = lax.broadcasted_iota(jnp.int32, (1, positions), 1)
    scores = jnp.where(position < lengths[b], scores, NEGATIVE_FLOOR)
    new_score = jnp.sum(q.astype(jnp.float32) * new_key, axis=1, keepdims=True) * scale
    top = jnp.maximum(jnp.max(scores, axis=1, keepdims=True), new_score)
    weights = jnp.exp(scores - top)
    new_weight = jnp.exp(new_score - top)
    total = jnp.sum(weights, axis=1, keepdims=True) + new_weight
    context = jnp.dot(
        weights.astype(jnp.bfloat16), cache[0, :, HD:], preferred_element_type=jnp.float32
    )
    context = context + new_weight.astype(jnp.bfloat16).astype(jnp.float32) * new_value
    context = context / total
    n_col = SIDE * SIDE
    for i in range(out.shape[0]):
        out[i, pl.ds(b, n_col, stride=8)] = context[
            n_col * (i // 2) : n_col * (i // 2 + 1), 128 * (i % 2) : 128 * (i % 2 + 1)
        ]


def attend(lengths, queries, new_kv, cache):
    rows_dev, heads, _ = queries.shape
    positions, wide = cache.shape[1:]
    n_col = SIDE * SIDE
    cols = heads // n_col * HD
    return pl.pallas_call(
        attend_kernel,
        grid_spec=pltpu.PrefetchScalarGridSpec(
            num_scalar_prefetch=1,
            grid=(rows_dev,),
            in_specs=[
                pl.BlockSpec((1, heads, HD), lambda b, _: (b, 0, 0)),
                pl.BlockSpec((rows_dev, wide), lambda b, _: (0, 0)),
                pl.BlockSpec((1, positions, wide), lambda b, _: (b, 0, 0)),
            ],
            out_specs=pl.BlockSpec((cols // 128, n_col * rows_dev, 128), lambda b, _: (0, 0, 0)),
        ),
        out_shape=jax.ShapeDtypeStruct((cols // 128, n_col * rows_dev, 128), jnp.float32),
        compiler_params=pltpu.CompilerParams(vmem_limit_bytes=VMEM_BYTES),
        name="attend",
    )(lengths, queries, new_kv, cache)


def output_kernel(
    ctx, wo, out, wbuf, crecv, allctx, pbuf, r1a, r1b, r2a, r2b, w_sem, cs, cr, ys, yr, gs, gr
):
    r, c = lax.axis_index("row"), lax.axis_index("col")
    x, z = c // SIDE, c % SIDE
    core = r % 2
    partner = r + 1 - 2 * core
    chunks, feats, lanes = out.shape
    half = 80
    n_col = SIDE * SIDE
    rows_dev = ctx.shape[1] // n_col

    load = pltpu.make_async_copy(wo, wbuf, w_sem)
    load.start()
    greet(
        [
            (n_col - 1, lambda d: (r, (c + 1 + d) % n_col)),
            (1, lambda d: (partner, c)),
            (3, lambda d: ((r + 2 * d + 2) % chunks, c)),
        ]
    )

    def row_send(d):
        to = (c + 1 + d) % n_col
        return rcopy(
            ctx.at[:, pl.ds(pl.multiple_of(to * rows_dev, 8), rows_dev)],
            crecv.at[:, pl.ds(pl.multiple_of(c * rows_dev, 8), rows_dev)],
            cs.at[d],
            cr.at[d],
            (r, to),
        )

    loop(0, n_col - 1, lambda d: row_send(d).start())
    mine = pl.ds(pl.multiple_of(c * rows_dev, 8), rows_dev)
    crecv[:, mine] = ctx[:, mine]
    loop(0, n_col - 1, lambda d: row_send(d).wait_recv())
    for i in range(crecv.shape[0]):
        allctx[0, :, 128 * i : 128 * (i + 1)] = crecv[i].astype(jnp.bfloat16)

    def y_send(d):
        step = jnp.where(d == 0, chunks - 2, jnp.where(d == 1, 2, 4))
        return rcopy(
            allctx.at[0], allctx.at[2 + 2 * d], ys.at[d], yr.at[d], ((r + step) % chunks, c)
        )

    def pass_on(d):
        return rcopy(
            allctx.at[2 + 2 * d], allctx.at[3 + 2 * d], ys.at[3 + d], yr.at[3 + d], (partner, c)
        )

    to_partner = rcopy(allctx.at[0], allctx.at[1], ys.at[6], yr.at[6], (partner, c))
    to_partner.start()
    loop(0, 3, lambda d: y_send(d).start())
    load.wait()

    def place(ax, i):
        return (i + SIDE) % SIDE

    def mid(ax):
        return x if ax == 0 else z

    def end(ax):
        return z if ax == 0 else x

    def group(ax, j, i, low, n):
        i = (i + SIDE) % SIDE
        return pbuf.at[j, i, pl.ds(low, n)] if ax == 0 else pbuf.at[j, pl.ds(low, n), i]

    def block(ax, j, i):
        i = (i + SIDE) % SIDE
        return pbuf.at[j, x, i] if ax == 0 else pbuf.at[j, i, z]

    def rows_of(ref, si):
        return ref.at[pl.ds(0, half)] if si == 0 else ref.at[pl.ds(half, feats - half)]

    def send_1a(ax, j, si):
        s = 1 - 2 * si
        return rcopy(
            group(ax, j, mid(ax) + 2, 2 * si, 2),
            r1a.at[j, si],
            gs.at[j, si],
            gr.at[j, si],
            (r, along(ax, x, z, s)),
        )

    def send_1b(ax, j, si):
        s = 1 - 2 * si
        return rcopy(
            group(ax, j, mid(ax) + s, 0, SIDE),
            r1b.at[j, si],
            gs.at[j, 2 + si],
            gr.at[j, 2 + si],
            (r, along(ax, x, z, s)),
        )

    def send_2a(ax, j, si):
        s = 1 - 2 * si
        return rcopy(
            rows_of(block(ax, j, end(ax) + 2), si),
            rows_of(r2a.at[j], si),
            gs.at[j, 4 + si],
            gr.at[j, 4 + si],
            (r, along(1 - ax, x, z, s)),
        )

    def send_2b(ax, j, si):
        s = 1 - 2 * si
        return rcopy(
            block(ax, j, end(ax) + s),
            r2b.at[j, si],
            gs.at[j, 6 + si],
            gr.at[j, 6 + si],
            (r, along(1 - ax, x, z, s)),
        )

    def both(p, do):
        for ax in (0, 1):
            do(ax, 2 * p + ax)

    def add_into(ref, *terms):
        total = ref[...].astype(jnp.float32)
        for term in terms:
            total = total + term[...].astype(jnp.float32)
        ref[...] = total.astype(jnp.bfloat16)

    def stage_1b(ax, j):
        for si in (0, 1):
            s = 1 - 2 * si
            send_1a(ax, j, si).wait_recv()
            add_into(group(ax, j, mid(ax) + s, 2 * si, 2), r1a.at[j, si])
            send_1b(ax, j, si).start()

    def stage_2a(ax, j):
        send_1b(ax, j, 0).wait_recv()
        send_1b(ax, j, 1).wait_recv()
        add_into(group(ax, j, mid(ax), 0, SIDE), r1b.at[j, 0], r1b.at[j, 1])
        for si in (0, 1):
            send_2a(ax, j, si).start()

    def stage_2b(ax, j):
        for si in (0, 1):
            s = 1 - 2 * si
            send_2a(ax, j, si).wait_recv()
            add_into(rows_of(block(ax, j, end(ax) + s), si), rows_of(r2a.at[j], si))
            send_2b(ax, j, si).start()

    def owner(j):
        step = jnp.where(j < 4, j // 2, jnp.where(j < 6, 3, 2))
        row = (r // 2 + step) % (chunks // 2)
        return 2 * row + (core + j) % 2

    def stage_end(ax, j):
        send_2b(ax, j, 0).wait_recv()
        send_2b(ax, j, 1).wait_recv()
        total = (
            block(ax, j, end(ax))[...].astype(jnp.float32)
            + r2b[j, 0].astype(jnp.float32)
            + r2b[j, 1].astype(jnp.float32)
        )
        out[owner(j)] = total.astype(jnp.bfloat16)

    def compute(j):
        term = jnp.dot(allctx[j], wbuf[...], preferred_element_type=jnp.float32)
        turned = term.astype(jnp.bfloat16).T
        for i in range(n_col):
            pbuf[j, i // SIDE, i % SIDE] = turned[feats * i : feats * (i + 1)]

    pairs = chunks // 2

    def step(t):
        @pl.when(t >= 4)
        def _():
            both(t - 4, stage_end)

        @pl.when(jnp.logical_and(t >= 3, t < pairs + 3))
        def _():
            both(t - 3, stage_2b)

        @pl.when(jnp.logical_and(t >= 2, t < pairs + 2))
        def _():
            both(t - 2, stage_2a)

        @pl.when(jnp.logical_and(t >= 1, t < pairs + 1))
        def _():
            both(t - 1, stage_1b)

        @pl.when(t < pairs)
        def _():
            compute(2 * t)
            for si in (0, 1):
                send_1a(0, 2 * t, si).start()

            @pl.when(t == 0)
            def _():
                to_partner.wait_recv()

            @pl.when(t > 0)
            def _():
                pass_on(t - 1).wait_recv()

            compute(2 * t + 1)
            for si in (0, 1):
                send_1a(1, 2 * t + 1, si).start()

        @pl.when(t < pairs - 1)
        def _():
            y_send(t).wait_recv()
            pass_on(t).start()

    loop(0, pairs + 4, step)

    def sent(p):
        for si in (0, 1):
            for send in (send_1a, send_1b, send_2a, send_2b):
                both(p, lambda ax, j: send(ax, j, si).wait_send())

    loop(0, pairs, sent)
    loop(0, n_col - 1, lambda d: row_send(d).wait_send())
    loop(0, 3, lambda d: y_send(d).wait_send())
    loop(0, 3, lambda d: pass_on(d).wait_send())
    to_partner.wait_send()


def project_out(context, weight, chunks, feats):
    rows, cols = context.shape[1], context.shape[0] * 128
    lanes = rows
    f32, bf16 = jnp.float32, jnp.bfloat16
    vmem = pl.BlockSpec(memory_space=pltpu.VMEM)
    anywhere = pl.BlockSpec(memory_space=pl.ANY)
    dma = pltpu.SemaphoreType.DMA
    n_col = SIDE * SIDE
    return pl.pallas_call(
        output_kernel,
        out_shape=jax.ShapeDtypeStruct((chunks, feats, lanes), bf16),
        in_specs=[vmem, anywhere],
        out_specs=vmem,
        scratch_shapes=[
            pltpu.VMEM(weight.shape, bf16),
            pltpu.VMEM(context.shape, f32),
            pltpu.VMEM((chunks, rows, cols), bf16),
            pltpu.VMEM((chunks, SIDE, SIDE, feats, lanes), bf16),
            pltpu.VMEM((chunks, 2, 2, feats, lanes), bf16),
            pltpu.VMEM((chunks, 2, SIDE, feats, lanes), bf16),
            pltpu.VMEM((chunks, feats, lanes), bf16),
            pltpu.VMEM((chunks, 2, feats, lanes), bf16),
            dma,
            dma((n_col - 1,)),
            dma((n_col - 1,)),
            dma((7,)),
            dma((7,)),
            dma((chunks, 8)),
            dma((chunks, 8)),
        ],
        compiler_params=pltpu.CompilerParams(
            collective_id=1, has_side_effects=True, vmem_limit_bytes=VMEM_BYTES
        ),
        name="project_out",
    )(context, weight)


def shards(
    tokens, layer_norm_gain, query_weight, kv_weight, output_weight_matrix, kv_cache, lengths
):
    chunks = lax.axis_size("row")
    devices = chunks * lax.axis_size("col")
    rows, feats = tokens.shape
    rows_dev = kv_cache.shape[0]
    heads = query_weight.shape[1] * lax.axis_size("col") // HD
    lanes = rows // chunks
    turned = tokens.reshape(chunks, lanes, feats).transpose(0, 2, 1)
    gain = jnp.pad(layer_norm_gain.astype(jnp.float32), (0, 8 * 128 - feats)).reshape(8, 128)
    queries, new_kv = project(
        turned, gain, query_weight, kv_weight, feats * devices, heads, rows_dev
    )
    context = attend(lengths, queries, new_kv.astype(jnp.float32), kv_cache)
    branch = project_out(context, output_weight_matrix, chunks, feats)
    branch = branch.transpose(0, 2, 1).reshape(rows, feats)
    return (branch, new_kv)


def solution(mesh):
    placed = (
        P(None, ("row", "col")),
        P(("row", "col")),
        P("row", "col"),
        P("row", None),
        P("col", "row"),
        P(("row", "col"), None, None),
        P(("row", "col")),
    )
    return jax.shard_map(
        shards,
        mesh=mesh,
        in_specs=placed,
        out_specs=(P(None, ("row", "col")), P(("row", "col"), None)),
        check_vma=False,
    )
```

```python
import functools

import jax
import jax.numpy as jnp
from jax import lax
from jax.experimental import pallas as pl
from jax.experimental.pallas import tpu as pltpu
from jax.sharding import PartitionSpec as P

MESH = pl.DeviceIdType.MESH
EPSILON = 1e-05
NEGATIVE_FLOOR = -1e30
HD = 256
SIDE = 4
N_COL = SIDE * SIDE
N_ROW = 8
QUARTERS = 4
ROWS_DEV = 8
LANES = 128
CHUNKS = 2 * QUARTERS
HALF = 80
ORDER = [
    ("first", 2), ("first", 1), ("first", 3), ("st_x", 0), ("first", 0), ("first_on", 2),
    ("first_on", 1), ("first_on", 3), ("st_z", 0), ("second", 2), ("second", 1), ("first_on", 0),
    ("st_y", 0), ("st_c", 0), ("second_on", 2), ("second_on", 1), ("second", 0), ("second", 3),
    ("st_end", 0), ("project", 2), ("sum_cores", 2), ("project", 1), ("sum_cores", 1), ("second_on", 0),
    ("rows_out", 2), ("second_on", 3), ("project", 0), ("rows_out", 1), ("sum_cores", 0), ("project", 3),
    ("attend", 2), ("sum_cores", 3), ("rows_out", 0), ("attend", 1), ("contexts_out", 2), ("rows_out", 3),
    ("attend", 0), ("contexts_out", 1), ("contexts_on", 2), ("project_out", 2), ("attend", 3), ("contexts_out", 0),
    ("contexts_on", 1), ("project_out", 1), ("sum_1b", 2), ("contexts_out", 3), ("contexts_on", 0), ("project_out", 0),
    ("sum_1b", 1), ("contexts_on", 3), ("sum_2a", 2), ("project_out", 3), ("sum_1b", 0), ("sum_1b", 3),
    ("sum_2a", 1), ("sum_2b", 2), ("sum_2a", 0), ("sum_2a", 3), ("sum_2b", 1), ("sum_end", 2),
    ("sum_2b", 0), ("sum_2b", 3), ("sum_end", 1), ("sum_end", 0), ("sum_end", 3),
]
VMEM_BYTES = 60 * 1024 * 1024
F32, BF16 = jnp.float32, jnp.bfloat16


def rcopy(src, dst, send_sem, recv_sem, device):
    return pltpu.make_async_remote_copy(
        src_ref=src,
        dst_ref=dst,
        send_sem=send_sem,
        recv_sem=recv_sem,
        device_id=device,
        device_id_type=MESH,
    )


def along(ax, x, z, step):
    if ax == 0:
        return ((x + step + SIDE) % SIDE) * SIDE + z
    return x * SIDE + (z + step + SIDE) % SIDE


def loop(low, high, body):
    def step(i, carry):
        body(i)
        return carry

    lax.fori_loop(low, high, step, 0)


def greet(peers):
    barrier = pltpu.get_barrier_semaphore()
    count = 0
    for number, device_of in peers:

        def hello(d, device_of=device_of):
            pl.semaphore_signal(barrier, inc=1, device_id=device_of(d), device_id_type=MESH)

        loop(0, number, hello)
        count += number
    pl.semaphore_wait(barrier, count)


def rows_of(ref, si):
    feats = ref.shape[0]
    return ref.at[pl.ds(0, HALF)] if si == 0 else ref.at[pl.ds(HALF, feats - HALF)]


def both(s, do):
    for ax in (0, 1):
        do(ax, 2 * s + ax)


def add_into(ref, *terms):
    total = ref[...].astype(F32)
    for term in terms:
        total = total + term[...].astype(F32)
    ref[...] = total.astype(BF16)


def kernel(
    n_features,
    tok,
    gain,
    wq,
    wkv,
    wo,
    cache,
    lengths,
    out,
    kv_out,
    perm,
    xbuf,
    qw,
    ow,
    kvc,
    gexp,
    xn,
    pq,
    pqr,
    yq,
    yqr,
    slab,
    slabr,
    cslab,
    cslabr,
    fold,
    cfold,
    qt,
    kvf,
    allctx,
    pbuf,
    r1a,
    r1b,
    r2a,
    r2b,
    ot,
    stx,
    stz,
    sty,
    stc,
    smsg,
    zmsg,
    ymsg,
    cmsg,
    mi,
    w_sem,
    k_sem,
    gs,
    gr,
    os_,
    or_,
    ps,
    pr,
    as_,
    ar,
    cs,
    cr,
    ss,
    sr,
):
    r, c = lax.axis_index("row"), lax.axis_index("col")
    x, z = c // SIDE, c % SIDE
    y, core = r // 2, r % 2
    partner = r + 1 - 2 * core
    feats = tok.shape[0]
    head_cols = wq.shape[1]
    q_parts = head_cols // LANES
    wide_parts = q_parts + 1
    wide = wide_parts * LANES
    block_rows = LANES // 4

    load_q = pltpu.make_async_copy(wq, qw.at[:, pl.ds(0, head_cols)], w_sem.at[0])
    load_kv = pltpu.make_async_copy(
        wkv.at[:, pl.ds(pl.multiple_of(x * LANES, LANES), LANES)],
        qw.at[:, pl.ds(head_cols, LANES)],
        w_sem.at[1],
    )
    load_o = pltpu.make_async_copy(wo, ow, w_sem.at[2])
    load_q.start()
    load_kv.start()

    def load_cache(b):
        return pltpu.make_async_copy(cache.at[b], kvc.at[b], k_sem.at[b])

    row = lax.broadcasted_iota(jnp.int32, (4 * LANES, LANES), 0)
    lane = lax.broadcasted_iota(jnp.int32, (4 * LANES, LANES), 1)
    same = jnp.logical_and(
        row // LANES == lane // block_rows, row % LANES // ROWS_DEV == lane % N_COL
    )
    bit = lane % block_rows // N_COL
    for s in range(QUARTERS):
        hit = jnp.logical_and(same, row % ROWS_DEV == 2 * s + bit)
        perm[s] = jnp.where(hit, 1.0, 0.0).astype(BF16)

    sums, squares = [], []
    for j in range(CHUNKS):
        s, h = j // 2, j % 2
        t = jnp.dot(
            tok[:, 4 * LANES * h : 4 * LANES * (h + 1)], perm[s], preferred_element_type=F32
        )
        xbuf[j, x, z] = t.astype(BF16)
        sums.append(jnp.sum(t, axis=0, keepdims=True))
        squares.append(jnp.sum(t * t, axis=0, keepdims=True))
    smsg[0:8] = jnp.concatenate(sums, axis=0)
    smsg[8:16] = jnp.concatenate(squares, axis=0)
    gains = gain[...].astype(F32)
    smsg[16:24] = jnp.zeros((8, LANES), F32)
    smsg[16:17] = gains[:, 0:LANES]
    smsg[17:18, 0 : feats - LANES] = gains[:, LANES:feats]
    stx[x] = smsg[...]

    fold[...] = jnp.zeros_like(fold)
    cfold[...] = jnp.zeros_like(cfold)
    greet(
        [
            (N_COL - 1, lambda d: (r, (c + 1 + d) % N_COL)),
            (1, lambda d: (partner, c)),
            (3, lambda d: ((r + 2 * d + 2) % N_ROW, c)),
        ]
    )

    def stat_x(d):
        return rcopy(smsg, stx.at[x], ss.at[d], sr.at[d], (r, along(0, x, z, d + 1)))

    def stat_z(d):
        return rcopy(zmsg, stz.at[z], ss.at[3 + d], sr.at[3 + d], (r, along(1, x, z, d + 1)))

    def stat_y(d):
        return rcopy(ymsg, sty.at[y], ss.at[6 + d], sr.at[6 + d], ((r + 2 * d + 2) % N_ROW, c))

    stat_c = rcopy(cmsg, stc.at[core], ss.at[9], sr.at[9], (partner, c))

    def mid(ax):
        return x if ax == 0 else z

    def end(ax):
        return z if ax == 0 else x

    def gblock(ax, j, i):
        i = (i + SIDE) % SIDE
        return xbuf.at[j, i, z] if ax == 0 else xbuf.at[j, x, i]

    def ggroup(ax, j, i, low, n):
        i = (i + SIDE) % SIDE
        return xbuf.at[j, pl.ds(low, n), i] if ax == 0 else xbuf.at[j, i, pl.ds(low, n)]

    def first(ax, j, si):
        here = gblock(ax, j, mid(ax))
        return rcopy(
            here, here, gs.at[j, si], gr.at[j, si], (r, along(ax, x, z, 1 - 2 * si))
        )

    def first_on(ax, j, si):
        s = 1 - 2 * si
        ref = rows_of(gblock(ax, j, mid(ax) - s), si)
        return rcopy(ref, ref, gs.at[j, 2 + si], gr.at[j, 2 + si], (r, along(ax, x, z, s)))

    def second(ax, j, si):
        ref = ggroup(ax, j, end(ax), 0, SIDE)
        to = (r, along(1 - ax, x, z, 1 - 2 * si))
        return rcopy(ref, ref, gs.at[j, 4 + si], gr.at[j, 4 + si], to)

    def second_on(ax, j, si):
        s = 1 - 2 * si
        ref = ggroup(ax, j, end(ax) - s, 2 * si, 2)
        return rcopy(ref, ref, gs.at[j, 6 + si], gr.at[j, 6 + si], (r, along(1 - ax, x, z, s)))

    def ways(s, do):
        for si in (0, 1):
            both(s, lambda ax, j: do(ax, j, si))

    loop(0, ROWS_DEV, lambda b: load_cache(b).start())
    load_o.start()

    def stats_x(s):
        loop(0, 3, lambda d: stat_x(d).start())

    def stats_z(s):
        loop(0, 3, lambda d: stat_x(d).wait_recv())
        zmsg[0:16] = stx[0, 0:16] + stx[1, 0:16] + stx[2, 0:16] + stx[3, 0:16]
        for i in range(SIDE):
            zmsg[16 + 8 * i : 24 + 8 * i] = stx[i, 16:24]
        stz[z] = zmsg[...]
        loop(0, 3, lambda d: stat_z(d).start())

    def spread(i):
        rows = stz[i % SIDE, pl.ds(pl.multiple_of(16 + 8 * (i // SIDE), 8), 8)]
        gexp[i, 0:128] = jnp.broadcast_to(rows[0:1], (128, 128)).T
        gexp[i, 128:feats] = jnp.broadcast_to(rows[1:2], (128, 128)).T[0 : feats - 128]

    def stats_y(s):
        loop(0, 3, lambda d: stat_z(d).wait_recv())
        ymsg[...] = stz[0, 0:16] + stz[1, 0:16] + stz[2, 0:16] + stz[3, 0:16]
        sty[y] = ymsg[...]
        loop(0, 3, lambda d: stat_y(d).start())
        loop(0, N_COL, spread)

    def stats_core(s):
        loop(0, 3, lambda d: stat_y(d).wait_recv())
        cmsg[...] = sty[0] + sty[1] + sty[2] + sty[3]
        stc[core] = cmsg[...]
        stat_c.start()

    def stats_end(s):
        stat_c.wait_recv()
        total = stc[0] + stc[1]
        average = total[0:8] / n_features
        mi[0:8] = average
        mi[8:16] = lax.rsqrt(total[8:16] / n_features - average * average + EPSILON)
        load_q.wait()
        load_kv.wait()
        load_o.wait()

    def tokens_first(s):
        ways(s, lambda ax, j, si: first(ax, j, si).start())

    def tokens_first_on(s):
        def do(ax, j, si):
            first(ax, j, si).wait_recv()
            first_on(ax, j, si).start()

        ways(s, do)

    def tokens_second(s):
        ways(s, lambda ax, j, si: first_on(ax, j, si).wait_recv())
        ways(s, lambda ax, j, si: second(ax, j, si).start())

    def tokens_second_on(s):
        def do(ax, j, si):
            second(ax, j, si).wait_recv()
            second_on(ax, j, si).start()

        ways(s, do)

    def to_partner(s):
        return rcopy(pq.at[s, 1 - core], pqr.at[s], ps.at[s, 0], pr.at[s, 0], (partner, c))

    def project(s):
        ways(s, lambda ax, j, si: second_on(ax, j, si).wait_recv())
        for h in (0, 1):
            j = 2 * s + h
            mean, inverse = mi[pl.ds(j, 1), :], mi[pl.ds(8 + j, 1), :]
            for i in range(N_COL):
                t = xbuf[j, i // SIDE, i % SIDE].astype(F32)
                xn[feats * i : feats * (i + 1), LANES * h : LANES * (h + 1)] = (
                    (t - mean) * inverse * gexp[i]
                ).astype(BF16)
        partial = lax.dot_general(
            xn[...], qw[...], (((0,), (0,)), ((), ())), preferred_element_type=F32
        ).astype(BF16)
        for i in range(N_ROW):
            pq[s, i % 2, i // 2] = partial[block_rows * i : block_rows * (i + 1)]
        to_partner(s).start()

    def to_y(s, d):
        to = (r + 2 * d + 2) % N_ROW
        return rcopy(
            yq.at[s, to // 2], yqr.at[s, y], ps.at[s, 1 + d], pr.at[s, 1 + d], (to, c)
        )

    def sum_cores(s):
        to_partner(s).wait_recv()
        yq[s] = (pq[s, core].astype(F32) + pqr[s].astype(F32)).astype(BF16)
        loop(0, 3, lambda d: to_y(s, d).start())
        yqr[s, y] = yq[s, y]

    def scatter(src, dst, send_sem, recv_sem, s, d):
        to = (c + 1 + d) % N_COL
        return rcopy(src.at[s, to], dst.at[s, c], send_sem.at[s, d], recv_sem.at[s, d], (r, to))

    def rows_out(s):
        loop(0, 3, lambda d: to_y(s, d).wait_recv())
        total = yqr[s, 0].astype(F32)
        for i in range(1, SIDE):
            total = total + yqr[s, i].astype(F32)
        for b in (0, 1):
            for k in range(wide_parts):
                fold[:, b * wide_parts + k, :] = total[
                    N_COL * b : N_COL * (b + 1), LANES * k : LANES * (k + 1)
                ]
        slab[s] = fold[...]
        loop(0, N_COL - 1, lambda d: scatter(slab, slabr, as_, ar, s, d).start())
        slabr[s, c] = fold[c]

    scale = HD**-0.5

    def attend(s):
        loop(0, N_COL - 1, lambda d: scatter(slab, slabr, as_, ar, s, d).wait_recv())
        fold[...] = slabr[s]
        for b in (0, 1):
            position = lax.broadcasted_iota(jnp.int32, (1, kvc.shape[1]), 1)
            n = 2 * s + b
            load_cache(n).wait()
            for k in range(q_parts):
                qt[N_COL * (k // 2) : N_COL * (k // 2 + 1), LANES * (k % 2) : LANES * (k % 2 + 1)] = (
                    fold[:, b * wide_parts + k, :].astype(BF16)
                )
            for i in range(SIDE):
                kvf[n, 0:1, LANES * i : LANES * (i + 1)] = (
                    fold[SIDE * i, b * wide_parts + q_parts : b * wide_parts + q_parts + 1, :]
                    .astype(BF16)
                    .astype(F32)
                )
            fresh = kvf[n, 0:1, :]
            new_key, new_value = fresh[:, :HD], fresh[:, HD:]
            q = qt[...]
            scores = (
                lax.dot_general(
                    q, kvc[n, :, :HD], (((1,), (1,)), ((), ())), preferred_element_type=F32
                )
                * scale
            )
            scores = jnp.where(position < lengths[n], scores, NEGATIVE_FLOOR)
            new_score = jnp.sum(q.astype(F32) * new_key, axis=1, keepdims=True) * scale
            top = jnp.maximum(jnp.max(scores, axis=1, keepdims=True), new_score)
            weights = jnp.exp(scores - top)
            new_weight = jnp.exp(new_score - top)
            total = jnp.sum(weights, axis=1, keepdims=True) + new_weight
            context = jnp.dot(weights.astype(BF16), kvc[n, :, HD:], preferred_element_type=F32)
            context = context + new_weight.astype(BF16).astype(F32) * new_value
            context = context / total
            for k in range(q_parts):
                cfold[:, b * q_parts + k, :] = context[
                    N_COL * (k // 2) : N_COL * (k // 2 + 1), LANES * (k % 2) : LANES * (k % 2 + 1)
                ]
        cslab[s] = cfold[...]
        loop(0, N_COL - 1, lambda d: scatter(cslab, cslabr, cs, cr, s, d).start())
        cslabr[s, c] = cfold[c]

    def share(s, d):
        to = ((r + 2 * d + 2) % N_ROW, c)
        ref = allctx.at[s, r]
        return rcopy(ref, ref, os_.at[s, d], or_.at[s, d], to)

    def pass_on(s, d):
        ref = allctx.at[s, (r + 2 * (SIDE - 1 - d)) % N_ROW]
        return rcopy(ref, ref, os_.at[s, 3 + d], or_.at[s, 3 + d], (partner, c))

    def share_core(s):
        ref = allctx.at[s, r]
        return rcopy(ref, ref, os_.at[s, 6], or_.at[s, 6], (partner, c))

    def contexts_out(s):
        loop(0, N_COL - 1, lambda d: scatter(cslab, cslabr, cs, cr, s, d).wait_recv())
        cfold[...] = cslabr[s]
        for b in (0, 1):
            for k in range(q_parts):
                allctx[s, r, N_COL * b : N_COL * (b + 1), LANES * k : LANES * (k + 1)] = cfold[
                    :, b * q_parts + k, :
                ].astype(BF16)
        loop(0, 3, lambda d: share(s, d).start())
        share_core(s).start()

    def contexts_on(s):
        def do(d):
            share(s, d).wait_recv()
            pass_on(s, d).start()

        loop(0, 3, do)

    def group(ax, j, i, low, n):
        i = (i + SIDE) % SIDE
        return pbuf.at[j, i, pl.ds(low, n)] if ax == 0 else pbuf.at[j, pl.ds(low, n), i]

    def block(ax, j, i):
        i = (i + SIDE) % SIDE
        return pbuf.at[j, x, i] if ax == 0 else pbuf.at[j, i, z]

    def send_1a(ax, j, si):
        src = group(ax, j, mid(ax) + 2, 2 * si, 2)
        to = (r, along(ax, x, z, 1 - 2 * si))
        return rcopy(src, r1a.at[j, si], gs.at[j, 8 + si], gr.at[j, 8 + si], to)

    def send_1b(ax, j, si):
        s = 1 - 2 * si
        src = group(ax, j, mid(ax) + s, 0, SIDE)
        to = (r, along(ax, x, z, s))
        return rcopy(src, r1b.at[j, si], gs.at[j, 10 + si], gr.at[j, 10 + si], to)

    def send_2a(ax, j, si):
        src = rows_of(block(ax, j, end(ax) + 2), si)
        to = (r, along(1 - ax, x, z, 1 - 2 * si))
        return rcopy(src, rows_of(r2a.at[j], si), gs.at[j, 12 + si], gr.at[j, 12 + si], to)

    def send_2b(ax, j, si):
        s = 1 - 2 * si
        src = block(ax, j, end(ax) + s)
        to = (r, along(1 - ax, x, z, s))
        return rcopy(src, r2b.at[j, si], gs.at[j, 14 + si], gr.at[j, 14 + si], to)

    def project_out(s):
        share_core(s).wait_recv()
        loop(0, 3, lambda d: pass_on(s, d).wait_recv())

        def do(ax, j):
            context = allctx[s, 4 * ax : 4 * ax + 4].reshape(LANES, head_cols)
            term = jnp.dot(context, ow[...], preferred_element_type=F32)
            turned = term.astype(BF16).T
            for i in range(N_COL):
                pbuf[j, i // SIDE, i % SIDE] = turned[feats * i : feats * (i + 1)]
            for si in (0, 1):
                send_1a(ax, j, si).start()

        both(s, do)

    def sum_1b(s):
        def do(ax, j):
            for si in (0, 1):
                send_1a(ax, j, si).wait_recv()
                add_into(group(ax, j, mid(ax) + 1 - 2 * si, 2 * si, 2), r1a.at[j, si])
                send_1b(ax, j, si).start()

        both(s, do)

    def sum_2a(s):
        def do(ax, j):
            send_1b(ax, j, 0).wait_recv()
            send_1b(ax, j, 1).wait_recv()
            add_into(group(ax, j, mid(ax), 0, SIDE), r1b.at[j, 0], r1b.at[j, 1])
            for si in (0, 1):
                send_2a(ax, j, si).start()

        both(s, do)

    def sum_2b(s):
        def do(ax, j):
            for si in (0, 1):
                send_2a(ax, j, si).wait_recv()
                add_into(
                    rows_of(block(ax, j, end(ax) + 1 - 2 * si), si), rows_of(r2a.at[j], si)
                )
                send_2b(ax, j, si).start()

        both(s, do)

    def sum_end(s):
        def do(ax, j):
            send_2b(ax, j, 0).wait_recv()
            send_2b(ax, j, 1).wait_recv()
            total = (
                block(ax, j, end(ax))[...].astype(F32)
                + r2b[j, 0].astype(F32)
                + r2b[j, 1].astype(F32)
            )
            ot[j] = total.astype(BF16)

        both(s, do)

    steps = dict(
        st_x=stats_x,
        st_z=stats_z,
        st_y=stats_y,
        st_c=stats_core,
        st_end=stats_end,
        first=tokens_first,
        first_on=tokens_first_on,
        second=tokens_second,
        second_on=tokens_second_on,
        project=project,
        sum_cores=sum_cores,
        rows_out=rows_out,
        attend=attend,
        contexts_out=contexts_out,
        contexts_on=contexts_on,
        project_out=project_out,
        sum_1b=sum_1b,
        sum_2a=sum_2a,
        sum_2b=sum_2b,
        sum_end=sum_end,
    )
    names = list(steps)
    order = []
    for name, s in ORDER:
        order.append((names.index(name), s))
    def take(step, s, low, high):
        if high - low == 1:
            steps[names[low]](s)
            return
        middle = (low + high) // 2
        pl.when(step < middle)(lambda: take(step, s, low, middle))
        pl.when(step >= middle)(lambda: take(step, s, middle, high))

    def in_order(t):
        code = jnp.int32(0)
        for i, (step, s) in enumerate(order):
            code = jnp.where(t == i, step * QUARTERS + s, code)
        take(code // QUARTERS, code % QUARTERS, 0, len(names))

    loop(0, len(order), in_order)

    for h in (0, 1):
        total = jnp.zeros((feats, 4 * LANES), F32)
        for s in range(QUARTERS):
            total = total + lax.dot_general(
                ot[2 * s + h], perm[s], (((1,), (1,)), ((), ())), preferred_element_type=F32
            )
        out[:, 4 * LANES * h : 4 * LANES * (h + 1)] = total.astype(BF16)
    fresh = [kvf[n, 0:1, :] for n in range(ROWS_DEV)]
    kv_out[...] = jnp.concatenate(fresh, axis=0).astype(BF16)

    loop(0, 3, lambda d: stat_x(d).wait_send())
    loop(0, 3, lambda d: stat_z(d).wait_send())
    loop(0, 3, lambda d: stat_y(d).wait_send())
    stat_c.wait_send()

    def sent(s):
        for send in (first, first_on, second, second_on, send_1a, send_1b, send_2a, send_2b):
            ways(s, lambda ax, j, si: send(ax, j, si).wait_send())
        to_partner(s).wait_send()
        loop(0, 3, lambda d: to_y(s, d).wait_send())
        loop(0, N_COL - 1, lambda d: scatter(slab, slabr, as_, ar, s, d).wait_send())
        loop(0, N_COL - 1, lambda d: scatter(cslab, cslabr, cs, cr, s, d).wait_send())
        loop(0, 3, lambda d: share(s, d).wait_send())
        loop(0, 3, lambda d: pass_on(s, d).wait_send())
        share_core(s).wait_send()

    loop(0, QUARTERS, sent)


def shards(
    tokens, layer_norm_gain, query_weight, kv_weight, output_weight_matrix, kv_cache, lengths
):
    devices = lax.axis_size("row") * lax.axis_size("col")
    rows, feats = tokens.shape
    depth, head_cols = query_weight.shape
    heads = head_cols * N_COL // HD
    kv_cols = kv_weight.shape[1]
    wide = head_cols + LANES
    block_rows = LANES // 4
    vmem = pl.BlockSpec(memory_space=pltpu.VMEM)
    smem = pl.BlockSpec(memory_space=pltpu.SMEM)
    anywhere = pl.BlockSpec(memory_space=pl.ANY)
    dma = pltpu.SemaphoreType.DMA
    slabs = pltpu.VMEM((QUARTERS, N_COL, 16, LANES), F32)
    branch, new_kv = pl.pallas_call(
        functools.partial(kernel, feats * devices),
        out_shape=(
            jax.ShapeDtypeStruct((feats, rows), BF16),
            jax.ShapeDtypeStruct((ROWS_DEV, kv_cols), BF16),
        ),
        in_specs=[vmem, vmem, anywhere, anywhere, anywhere, anywhere, smem],
        out_specs=(vmem, vmem),
        scratch_shapes=[
            pltpu.VMEM((QUARTERS, 4 * LANES, LANES), BF16),
            pltpu.VMEM((CHUNKS, SIDE, SIDE, feats, LANES), BF16),
            pltpu.VMEM((depth, wide), BF16),
            pltpu.VMEM(output_weight_matrix.shape, BF16),
            pltpu.VMEM(kv_cache.shape, BF16),
            pltpu.VMEM((N_COL, feats, LANES), F32),
            pltpu.VMEM((depth, 2 * LANES), BF16),
            pltpu.VMEM((QUARTERS, 2, SIDE, block_rows, wide), BF16),
            pltpu.VMEM((QUARTERS, SIDE, block_rows, wide), BF16),
            pltpu.VMEM((QUARTERS, SIDE, block_rows, wide), BF16),
            pltpu.VMEM((QUARTERS, SIDE, block_rows, wide), BF16),
            slabs,
            slabs,
            slabs,
            slabs,
            pltpu.VMEM((N_COL, 16, LANES), F32),
            pltpu.VMEM((N_COL, 16, LANES), F32),
            pltpu.VMEM((heads, HD), BF16),
            pltpu.VMEM((ROWS_DEV, 8, kv_cols), F32),
            pltpu.VMEM((QUARTERS, N_ROW, block_rows, head_cols), BF16),
            pltpu.VMEM((CHUNKS, SIDE, SIDE, feats, LANES), BF16),
            pltpu.VMEM((CHUNKS, 2, 2, feats, LANES), BF16),
            pltpu.VMEM((CHUNKS, 2, SIDE, feats, LANES), BF16),
            pltpu.VMEM((CHUNKS, feats, LANES), BF16),
            pltpu.VMEM((CHUNKS, 2, feats, LANES), BF16),
            pltpu.VMEM((CHUNKS, feats, LANES), BF16),
            pltpu.VMEM((SIDE, 24, LANES), F32),
            pltpu.VMEM((SIDE, 48, LANES), F32),
            pltpu.VMEM((SIDE, 16, LANES), F32),
            pltpu.VMEM((2, 16, LANES), F32),
            pltpu.VMEM((24, LANES), F32),
            pltpu.VMEM((48, LANES), F32),
            pltpu.VMEM((16, LANES), F32),
            pltpu.VMEM((16, LANES), F32),
            pltpu.VMEM((16, LANES), F32),
            dma((3,)),
            dma((ROWS_DEV,)),
            dma((CHUNKS, 16)),
            dma((CHUNKS, 16)),
            dma((QUARTERS, 7)),
            dma((QUARTERS, 7)),
            dma((QUARTERS, 4)),
            dma((QUARTERS, 4)),
            dma((QUARTERS, N_COL - 1)),
            dma((QUARTERS, N_COL - 1)),
            dma((QUARTERS, N_COL - 1)),
            dma((QUARTERS, N_COL - 1)),
            dma((10,)),
            dma((10,)),
        ],
        compiler_params=pltpu.CompilerParams(
            collective_id=0, has_side_effects=True, vmem_limit_bytes=VMEM_BYTES
        ),
        name="decode",
    )(
        tokens.T,
        layer_norm_gain.reshape(1, feats),
        query_weight,
        kv_weight,
        output_weight_matrix,
        kv_cache,
        lengths,
    )
    return branch.T, new_kv


def solution(mesh):
    placed = (
        P(None, ("row", "col")),
        P(("row", "col")),
        P("row", "col"),
        P("row", None),
        P("col", "row"),
        P(("row", "col"), None, None),
        P(("row", "col")),
    )
    return jax.shard_map(
        shards,
        mesh=mesh,
        in_specs=placed,
        out_specs=(P(None, ("row", "col")), P(("row", "col"), None)),
        check_vma=False,
    )
```

```python
import functools

import jax
import jax.numpy as jnp
from jax import lax
from jax.experimental import pallas as pl
from jax.experimental.pallas import tpu as pltpu
from jax.sharding import PartitionSpec as P

MESH = pl.DeviceIdType.MESH
EPSILON = 1e-05
NEGATIVE_FLOOR = -1e30
HD = 256
SIDE = 4
N_COL = SIDE * SIDE
N_ROW = 8
QUARTERS = 4
ROWS_DEV = 8
LANES = 128
CHUNKS = 2 * QUARTERS
HALF = 80
ORDER = [
    ("first", 3), ("first", 1), ("first", 0), ("first", 2), ("st_x", 0), ("first_on", 3),
    ("first_on", 0), ("first_on", 1), ("first_on", 2), ("st_z", 0), ("second", 3), ("second", 1),
    ("st_y", 0), ("second_on", 3), ("second", 0), ("second_on", 1), ("st_c", 0), ("second", 2),
    ("st_end", 0), ("project", 3), ("sum_cores", 3), ("second_on", 0), ("project", 1), ("sum_cores", 1),
    ("rows_out", 3), ("second_on", 2), ("project", 0), ("sum_cores", 0), ("rows_out", 1), ("project", 2),
    ("attend", 3), ("sum_cores", 2), ("rows_out", 0), ("attend", 1), ("contexts_out", 3), ("rows_out", 2),
    ("attend", 0), ("contexts_out", 1), ("contexts_on", 3), ("project_out", 3), ("attend", 2), ("contexts_out", 0),
    ("contexts_on", 1), ("project_out", 1), ("sum_1b", 3), ("contexts_out", 2), ("contexts_on", 0), ("project_out", 0),
    ("sum_1b", 1), ("contexts_on", 2), ("project_out", 2), ("sum_1b", 0), ("sum_1b", 2), ("sum_2a", 1),
    ("sum_2a", 0), ("sum_2a", 3), ("sum_2a", 2), ("sum_2b", 1), ("sum_2b", 0), ("sum_2b", 3),
    ("sum_2b", 2), ("sum_end", 1), ("sum_end", 3), ("sum_end", 0), ("sum_end", 2),
]
VMEM_BYTES = 60 * 1024 * 1024
F32, BF16 = jnp.float32, jnp.bfloat16


def rcopy(src, dst, send_sem, recv_sem, device):
    return pltpu.make_async_remote_copy(
        src_ref=src,
        dst_ref=dst,
        send_sem=send_sem,
        recv_sem=recv_sem,
        device_id=device,
        device_id_type=MESH,
    )


def along(ax, x, z, step):
    if ax == 0:
        return ((x + step + SIDE) % SIDE) * SIDE + z
    return x * SIDE + (z + step + SIDE) % SIDE


def loop(low, high, body):
    def step(i, carry):
        body(i)
        return carry

    lax.fori_loop(low, high, step, 0)


def landed(ref, sem):
    pltpu.make_async_copy(ref, ref, sem).wait()


def greet(peers):
    barrier = pltpu.get_barrier_semaphore()
    count = 0
    for number, device_of in peers:

        def hello(d, device_of=device_of):
            pl.semaphore_signal(barrier, inc=1, device_id=device_of(d), device_id_type=MESH)

        loop(0, number, hello)
        count += number
    return count


def rows_of(ref, si):
    feats = ref.shape[0]
    return ref.at[pl.ds(0, HALF)] if si == 0 else ref.at[pl.ds(HALF, feats - HALF)]


def both(s, do):
    for ax in (0, 1):
        do(ax, 2 * s + ax)


def add_into(ref, *terms):
    total = ref[...].astype(F32)
    for term in terms:
        total = total + term[...].astype(F32)
    ref[...] = total.astype(BF16)


def kernel(
    n_features,
    tok,
    gain,
    wq,
    wkv,
    wo,
    cache,
    lengths,
    out,
    kv_out,
    perm,
    xbuf,
    qw,
    ow,
    kvc,
    gexp,
    xn,
    pq,
    pqr,
    yq,
    yqr,
    slab,
    slabr,
    cslab,
    cslabr,
    fold,
    cfold,
    qt,
    kvf,
    allctx,
    pbuf,
    r1a,
    r1b,
    r2a,
    r2b,
    ot,
    stx,
    stz,
    sty,
    stc,
    smsg,
    zmsg,
    ymsg,
    cmsg,
    mi,
    w_sem,
    k_sem,
    gs,
    gr,
    os_,
    or_,
    ps,
    pr,
    as_,
    ar,
    cs,
    cr,
    ss,
    sr,
):
    r, c = lax.axis_index("row"), lax.axis_index("col")
    x, z = c // SIDE, c % SIDE
    y, core = r // 2, r % 2
    partner = r + 1 - 2 * core
    feats = tok.shape[0]
    head_cols = wq.shape[1]
    q_parts = head_cols // LANES
    wide_parts = q_parts + 1
    wide = wide_parts * LANES
    block_rows = LANES // 4

    peers = greet(
        [
            (N_COL - 1, lambda d: (r, (c + 1 + d) % N_COL)),
            (1, lambda d: (partner, c)),
            (3, lambda d: ((r + 2 * d + 2) % N_ROW, c)),
        ]
    )

    load_q = pltpu.make_async_copy(wq, qw.at[:, pl.ds(0, head_cols)], w_sem.at[0])
    load_kv = pltpu.make_async_copy(
        wkv.at[:, pl.ds(pl.multiple_of(x * LANES, LANES), LANES)],
        qw.at[:, pl.ds(head_cols, LANES)],
        w_sem.at[1],
    )
    load_o = pltpu.make_async_copy(wo, ow, w_sem.at[2])
    load_q.start()
    load_kv.start()

    def load_cache(b):
        return pltpu.make_async_copy(cache.at[b], kvc.at[b], k_sem.at[b])

    loop(0, ROWS_DEV, lambda b: load_cache(b).start())
    load_o.start()

    row = lax.broadcasted_iota(jnp.int32, (4 * LANES, LANES), 0)
    lane = lax.broadcasted_iota(jnp.int32, (4 * LANES, LANES), 1)
    same = jnp.logical_and(
        row // LANES == lane // block_rows, row % LANES // ROWS_DEV == lane % N_COL
    )
    bit = lane % block_rows // N_COL
    for s in range(QUARTERS):
        hit = jnp.logical_and(same, row % ROWS_DEV == 2 * s + bit)
        perm[s] = jnp.where(hit, 1.0, 0.0).astype(BF16)

    sums, squares = [], []
    for j in range(CHUNKS):
        s, h = j // 2, j % 2
        t = jnp.dot(
            tok[:, 4 * LANES * h : 4 * LANES * (h + 1)], perm[s], preferred_element_type=F32
        )
        xbuf[j, x, z] = t.astype(BF16)
        sums.append(jnp.sum(t, axis=0, keepdims=True))
        squares.append(jnp.sum(t * t, axis=0, keepdims=True))
    smsg[0:8] = jnp.concatenate(sums, axis=0)
    smsg[8:16] = jnp.concatenate(squares, axis=0)
    gains = gain[...].astype(F32).reshape(1, feats)
    smsg[16:24] = jnp.zeros((8, LANES), F32)
    smsg[16:17] = gains[:, 0:LANES]
    smsg[17:18, 0 : feats - LANES] = gains[:, LANES:feats]
    stx[x] = smsg[...]

    fold[...] = jnp.zeros_like(fold)
    cfold[...] = jnp.zeros_like(cfold)
    pl.semaphore_wait(pltpu.get_barrier_semaphore(), peers)

    def stat_x(d):
        return rcopy(smsg, stx.at[x], ss.at[0], sr.at[0], (r, along(0, x, z, d + 1)))

    def stat_z(d):
        return rcopy(zmsg, stz.at[z], ss.at[1], sr.at[1], (r, along(1, x, z, d + 1)))

    def stat_y(d):
        return rcopy(ymsg, sty.at[y], ss.at[2], sr.at[2], ((r + 2 * d + 2) % N_ROW, c))

    stat_c = rcopy(cmsg, stc.at[core], ss.at[3], sr.at[3], (partner, c))

    def mid(ax):
        return x if ax == 0 else z

    def end(ax):
        return z if ax == 0 else x

    def gblock(ax, j, i):
        i = (i + SIDE) % SIDE
        return xbuf.at[j, i, z] if ax == 0 else xbuf.at[j, x, i]

    def ggroup(ax, j, i, low, n):
        i = (i + SIDE) % SIDE
        return xbuf.at[j, pl.ds(low, n), i] if ax == 0 else xbuf.at[j, i, pl.ds(low, n)]

    def first(ax, j, si):
        here = gblock(ax, j, mid(ax))
        return rcopy(
            here, here, gs.at[j // 2, 0], gr.at[j // 2, 0], (r, along(ax, x, z, 1 - 2 * si))
        )

    def first_on(ax, j, si):
        s = 1 - 2 * si
        ref = rows_of(gblock(ax, j, mid(ax) - s), si)
        return rcopy(ref, ref, gs.at[j // 2, 1], gr.at[j // 2, 1], (r, along(ax, x, z, s)))

    def second(ax, j, si):
        ref = ggroup(ax, j, end(ax), 0, SIDE)
        to = (r, along(1 - ax, x, z, 1 - 2 * si))
        return rcopy(ref, ref, gs.at[j // 2, 2], gr.at[j // 2, 2], to)

    def second_on(ax, j, si):
        s = 1 - 2 * si
        ref = ggroup(ax, j, end(ax) - s, 2 * si, 2)
        return rcopy(ref, ref, gs.at[j // 2, 3], gr.at[j // 2, 3], (r, along(1 - ax, x, z, s)))

    def ways(s, do):
        for si in (0, 1):
            both(s, lambda ax, j: do(ax, j, si))

    def stats_x(s):
        loop(0, 3, lambda d: stat_x(d).start())

    def stats_z(s):
        landed(stx.at[pl.ds(0, 3)], sr.at[0])
        zmsg[0:16] = stx[0, 0:16] + stx[1, 0:16] + stx[2, 0:16] + stx[3, 0:16]
        for i in range(SIDE):
            zmsg[16 + 8 * i : 24 + 8 * i] = stx[i, 16:24]
        stz[z] = zmsg[...]
        loop(0, 3, lambda d: stat_z(d).start())

    def spread(i):
        rows = stz[i % SIDE, pl.ds(pl.multiple_of(16 + 8 * (i // SIDE), 8), 8)]
        gexp[i, 0:128] = jnp.broadcast_to(rows[0:1], (128, 128)).T
        gexp[i, 128:feats] = jnp.broadcast_to(rows[1:2], (128, 128)).T[0 : feats - 128]

    def stats_y(s):
        landed(stz.at[pl.ds(0, 3)], sr.at[1])
        ymsg[...] = stz[0, 0:16] + stz[1, 0:16] + stz[2, 0:16] + stz[3, 0:16]
        sty[y] = ymsg[...]
        loop(0, 3, lambda d: stat_y(d).start())
        loop(0, N_COL, spread)

    def stats_core(s):
        landed(sty.at[pl.ds(0, 3)], sr.at[2])
        cmsg[...] = sty[0] + sty[1] + sty[2] + sty[3]
        stc[core] = cmsg[...]
        stat_c.start()

    def stats_end(s):
        stat_c.wait_recv()
        total = stc[0] + stc[1]
        average = total[0:8] / n_features
        mi[0:8] = average
        mi[8:16] = lax.rsqrt(total[8:16] / n_features - average * average + EPSILON)
        load_q.wait()
        load_kv.wait()
        load_o.wait()

    def tokens_first(s):
        ways(s, lambda ax, j, si: first(ax, j, si).start())

    def tokens_first_on(s):
        landed(xbuf.at[2 * s, 0], gr.at[s, 0])
        ways(s, lambda ax, j, si: first_on(ax, j, si).start())

    def tokens_second(s):
        landed(xbuf.at[2 * s, 0, pl.ds(0, 2)], gr.at[s, 1])
        ways(s, lambda ax, j, si: second(ax, j, si).start())

    def tokens_second_on(s):
        landed(xbuf.at[2 * s], gr.at[s, 2])
        ways(s, lambda ax, j, si: second_on(ax, j, si).start())

    def to_partner(s):
        return rcopy(pq.at[s, 1 - core], pqr.at[s], ps.at[s, 0], pr.at[s, 0], (partner, c))

    def project(s):
        landed(xbuf.at[2 * s, pl.ds(0, 2)], gr.at[s, 3])
        for h in (0, 1):
            j = 2 * s + h
            mean, inverse = mi[pl.ds(j, 1), :], mi[pl.ds(8 + j, 1), :]
            for i in range(N_COL):
                t = xbuf[j, i // SIDE, i % SIDE].astype(F32)
                xn[feats * i : feats * (i + 1), LANES * h : LANES * (h + 1)] = (
                    (t - mean) * inverse * gexp[i]
                ).astype(BF16)
        partial = lax.dot_general(
            xn[...], qw[...], (((0,), (0,)), ((), ())), preferred_element_type=F32
        ).astype(BF16)
        for i in range(N_ROW):
            pq[s, i % 2, i // 2] = partial[block_rows * i : block_rows * (i + 1)]
        to_partner(s).start()

    def to_y(s, d):
        to = (r + 2 * d + 2) % N_ROW
        return rcopy(
            yq.at[s, to // 2], yqr.at[s, y], ps.at[s, 1], pr.at[s, 1], (to, c)
        )

    def sum_cores(s):
        to_partner(s).wait_recv()
        yq[s] = (pq[s, core].astype(F32) + pqr[s].astype(F32)).astype(BF16)
        loop(0, 3, lambda d: to_y(s, d).start())
        yqr[s, y] = yq[s, y]

    def scatter(src, dst, send_sem, recv_sem, s, d):
        to = (c + 1 + d) % N_COL
        return rcopy(src.at[s, to], dst.at[s, c], send_sem.at[s], recv_sem.at[s], (r, to))

    def rows_out(s):
        landed(yqr.at[s, pl.ds(0, 3)], pr.at[s, 1])
        total = yqr[s, 0].astype(F32)
        for i in range(1, SIDE):
            total = total + yqr[s, i].astype(F32)
        for b in (0, 1):
            for k in range(wide_parts):
                fold[:, b * wide_parts + k, :] = total[
                    N_COL * b : N_COL * (b + 1), LANES * k : LANES * (k + 1)
                ]
        slab[s] = fold[...].astype(BF16)
        loop(0, N_COL - 1, lambda d: scatter(slab, slabr, as_, ar, s, d).start())
        slabr[s, c] = slab[s, c]

    scale = HD**-0.5

    def attend(s):
        landed(slabr.at[s, pl.ds(0, N_COL - 1)], ar.at[s])
        fold[...] = slabr[s].astype(F32)
        position = lax.broadcasted_iota(jnp.int32, (1, kvc.shape[1]), 1)
        rows = []
        for b in (0, 1):
            for k in range(q_parts):
                at = slice(N_COL * (k // 2), N_COL * (k // 2 + 1))
                qt[b, at, LANES * (k % 2) : LANES * (k % 2 + 1)] = fold[
                    :, b * wide_parts + k, :
                ].astype(BF16)
            for i in range(SIDE):
                k = b * wide_parts + q_parts
                kvf[2 * s + b, 0:1, LANES * i : LANES * (i + 1)] = fold[SIDE * i, k : k + 1, :]
        for b in (0, 1):
            n = 2 * s + b
            load_cache(n).wait()
            q, new_key = qt[b], kvf[n, 0:1, :HD]
            scores = (
                lax.dot_general(
                    q, kvc[n, :, :HD], (((1,), (1,)), ((), ())), preferred_element_type=F32
                )
                * scale
            )
            scores = jnp.where(position < lengths[n], scores, NEGATIVE_FLOOR)
            new_score = jnp.sum(q.astype(F32) * new_key, axis=1, keepdims=True) * scale
            rows.append((n, scores, new_score))
        weighed = []
        for n, scores, new_score in rows:
            top = jnp.maximum(jnp.max(scores, axis=1, keepdims=True), new_score)
            weights = jnp.exp(scores - top)
            new_weight = jnp.exp(new_score - top)
            total = jnp.sum(weights, axis=1, keepdims=True) + new_weight
            weighed.append((n, weights.astype(BF16), new_weight, total))
        for b, (n, weights, new_weight, total) in enumerate(weighed):
            new_value = kvf[n, 0:1, HD:]
            context = jnp.dot(weights, kvc[n, :, HD:], preferred_element_type=F32)
            context = context + new_weight.astype(BF16).astype(F32) * new_value
            context = context / total
            for k in range(q_parts):
                cfold[:, b * q_parts + k, :] = context[
                    N_COL * (k // 2) : N_COL * (k // 2 + 1), LANES * (k % 2) : LANES * (k % 2 + 1)
                ]
        cslab[s] = cfold[...].astype(BF16)
        loop(0, N_COL - 1, lambda d: scatter(cslab, cslabr, cs, cr, s, d).start())
        cslabr[s, c] = cslab[s, c]

    def share(s, d):
        to = ((r + 2 * d + 2) % N_ROW, c)
        ref = allctx.at[s, r]
        return rcopy(ref, ref, os_.at[s], or_.at[s, d], to)

    def pass_on(s, d):
        ref = allctx.at[s, (r + 2 * (SIDE - 1 - d)) % N_ROW]
        return rcopy(ref, ref, os_.at[s], or_.at[s, 3], (partner, c))

    def share_core(s):
        ref = allctx.at[s, r]
        return rcopy(ref, ref, os_.at[s], or_.at[s, 3], (partner, c))

    def contexts_out(s):
        landed(cslabr.at[s, pl.ds(0, N_COL - 1)], cr.at[s])
        cfold[...] = cslabr[s].astype(F32)
        for b in (0, 1):
            for k in range(q_parts):
                allctx[s, r, N_COL * b : N_COL * (b + 1), LANES * k : LANES * (k + 1)] = cfold[
                    :, b * q_parts + k, :
                ].astype(BF16)
        loop(0, 3, lambda d: share(s, d).start())
        share_core(s).start()

    def contexts_on(s):
        def do(d):
            share(s, d).wait_recv()
            pass_on(s, d).start()

        loop(0, 3, do)

    def group(ax, j, i, low, n):
        i = (i + SIDE) % SIDE
        return pbuf.at[j, i, pl.ds(low, n)] if ax == 0 else pbuf.at[j, pl.ds(low, n), i]

    def block(ax, j, i):
        i = (i + SIDE) % SIDE
        return pbuf.at[j, x, i] if ax == 0 else pbuf.at[j, i, z]

    def send_1a(ax, j, si):
        src = group(ax, j, mid(ax) + 2, 2 * si, 2)
        to = (r, along(ax, x, z, 1 - 2 * si))
        return rcopy(src, r1a.at[j, si], gs.at[j // 2, 4], gr.at[j // 2, 4], to)

    def send_1b(ax, j, si):
        s = 1 - 2 * si
        src = group(ax, j, mid(ax) + s, 0, SIDE)
        to = (r, along(ax, x, z, s))
        return rcopy(src, r1b.at[j, si], gs.at[j // 2, 5], gr.at[j // 2, 5], to)

    def send_2a(ax, j, si):
        src = rows_of(block(ax, j, end(ax) + 2), si)
        to = (r, along(1 - ax, x, z, 1 - 2 * si))
        return rcopy(src, rows_of(r2a.at[j], si), gs.at[j // 2, 6], gr.at[j // 2, 6], to)

    def send_2b(ax, j, si):
        s = 1 - 2 * si
        src = block(ax, j, end(ax) + s)
        to = (r, along(1 - ax, x, z, s))
        return rcopy(src, r2b.at[j, si], gs.at[j // 2, 7], gr.at[j // 2, 7], to)

    def project_out(s):
        landed(allctx.at[s, pl.ds(0, 4)], or_.at[s, 3])

        def do(ax, j):
            context = allctx[s, 4 * ax : 4 * ax + 4].reshape(LANES, head_cols)
            term = jnp.dot(context, ow[...], preferred_element_type=F32)
            turned = term.astype(BF16).T
            for i in range(N_COL):
                pbuf[j, i // SIDE, i % SIDE] = turned[feats * i : feats * (i + 1)]
            for si in (0, 1):
                send_1a(ax, j, si).start()

        both(s, do)

    def sum_1b(s):
        landed(pbuf.at[2 * s, pl.ds(0, 2)], gr.at[s, 4])

        def do(ax, j):
            for si in (0, 1):
                add_into(group(ax, j, mid(ax) + 1 - 2 * si, 2 * si, 2), r1a.at[j, si])
                send_1b(ax, j, si).start()

        both(s, do)

    def sum_2a(s):
        landed(pbuf.at[2 * s], gr.at[s, 5])

        def do(ax, j):
            add_into(group(ax, j, mid(ax), 0, SIDE), r1b.at[j, 0], r1b.at[j, 1])
            for si in (0, 1):
                send_2a(ax, j, si).start()

        both(s, do)

    def sum_2b(s):
        landed(pbuf.at[2 * s, 0, pl.ds(0, 2)], gr.at[s, 6])

        def do(ax, j):
            for si in (0, 1):
                add_into(
                    rows_of(block(ax, j, end(ax) + 1 - 2 * si), si), rows_of(r2a.at[j], si)
                )
                send_2b(ax, j, si).start()

        both(s, do)

    def sum_end(s):
        landed(pbuf.at[2 * s, 0], gr.at[s, 7])

        def do(ax, j):
            total = (
                block(ax, j, end(ax))[...].astype(F32)
                + r2b[j, 0].astype(F32)
                + r2b[j, 1].astype(F32)
            )
            ot[j] = total.astype(BF16)

        both(s, do)

    steps = dict(
        st_x=stats_x,
        st_z=stats_z,
        st_y=stats_y,
        st_c=stats_core,
        st_end=stats_end,
        first=tokens_first,
        first_on=tokens_first_on,
        second=tokens_second,
        second_on=tokens_second_on,
        project=project,
        sum_cores=sum_cores,
        rows_out=rows_out,
        attend=attend,
        contexts_out=contexts_out,
        contexts_on=contexts_on,
        project_out=project_out,
        sum_1b=sum_1b,
        sum_2a=sum_2a,
        sum_2b=sum_2b,
        sum_end=sum_end,
    )
    names = list(steps)
    order = []
    for name, s in ORDER:
        order.append((names.index(name), s))
    def take(step, s, low, high):
        if high - low == 1:
            steps[names[low]](s)
            return
        middle = (low + high) // 2
        pl.when(step < middle)(lambda: take(step, s, low, middle))
        pl.when(step >= middle)(lambda: take(step, s, middle, high))

    def in_order(t):
        code = jnp.int32(0)
        for i, (step, s) in enumerate(order):
            code = jnp.where(t == i, step * QUARTERS + s, code)
        take(code // QUARTERS, code % QUARTERS, 0, len(names))

    loop(0, len(order), in_order)

    for h in (0, 1):
        total = jnp.zeros((feats, 4 * LANES), F32)
        for s in range(QUARTERS):
            total = total + lax.dot_general(
                ot[2 * s + h], perm[s], (((1,), (1,)), ((), ())), preferred_element_type=F32
            )
        out[:, 4 * LANES * h : 4 * LANES * (h + 1)] = total.astype(BF16)
    fresh = [kvf[n, 0:1, :] for n in range(ROWS_DEV)]
    kv_out[...] = jnp.concatenate(fresh, axis=0).astype(BF16)

    landed(stx.at[pl.ds(0, 3)], ss.at[0])
    landed(stz.at[pl.ds(0, 3)], ss.at[1])
    landed(sty.at[pl.ds(0, 3)], ss.at[2])
    stat_c.wait_send()

    def sent(s):
        for k, buf in ((0, xbuf), (4, pbuf)):
            both_ways = (buf.at[2 * s, pl.ds(0, 2)], buf.at[2 * s])
            part, whole = buf.at[2 * s, 0, pl.ds(0, 2)], buf.at[2 * s, 0]
            sizes = (whole, part, both_ways[1], both_ways[0])
            sizes = sizes if k == 0 else (both_ways[0], both_ways[1], part, whole)
            for i, ref in enumerate(sizes):
                landed(ref, gs.at[s, k + i])
        to_partner(s).wait_send()
        landed(yqr.at[s, pl.ds(0, 3)], ps.at[s, 1])
        landed(slab.at[s, pl.ds(0, N_COL - 1)], as_.at[s])
        landed(cslab.at[s, pl.ds(0, N_COL - 1)], cs.at[s])
        landed(allctx.at[s, pl.ds(0, 7)], os_.at[s])

    loop(0, QUARTERS, sent)


def hand_over_kernel(branch, new_kv, branch_out, new_kv_out):
    branch_out[...] = branch[...]
    new_kv_out[...] = new_kv[...]


def hand_over(branch, new_kv):
    vmem = pl.BlockSpec(memory_space=pltpu.VMEM)
    return pl.pallas_call(
        hand_over_kernel,
        out_shape=(
            jax.ShapeDtypeStruct(branch.shape, branch.dtype),
            jax.ShapeDtypeStruct(new_kv.shape, new_kv.dtype),
        ),
        in_specs=[vmem, vmem],
        out_specs=(vmem, vmem),
        name="hand_over",
    )(branch, new_kv)


def shards(
    tokens, layer_norm_gain, query_weight, kv_weight, output_weight_matrix, kv_cache, lengths
):
    devices = lax.axis_size("row") * lax.axis_size("col")
    rows, feats = tokens.shape
    depth, head_cols = query_weight.shape
    heads = head_cols * N_COL // HD
    kv_cols = kv_weight.shape[1]
    wide = head_cols + LANES
    block_rows = LANES // 4
    vmem = pl.BlockSpec(memory_space=pltpu.VMEM)
    smem = pl.BlockSpec(memory_space=pltpu.SMEM)
    anywhere = pl.BlockSpec(memory_space=pl.ANY)
    dma = pltpu.SemaphoreType.DMA
    slabs = pltpu.VMEM((QUARTERS, N_COL, 16, LANES), BF16)
    branch, new_kv = pl.pallas_call(
        functools.partial(kernel, feats * devices),
        out_shape=(
            jax.ShapeDtypeStruct((feats, rows), BF16),
            jax.ShapeDtypeStruct((ROWS_DEV, kv_cols), BF16),
        ),
        in_specs=[vmem, vmem, anywhere, anywhere, anywhere, anywhere, smem],
        out_specs=(vmem, vmem),
        scratch_shapes=[
            pltpu.VMEM((QUARTERS, 4 * LANES, LANES), BF16),
            pltpu.VMEM((CHUNKS, SIDE, SIDE, feats, LANES), BF16),
            pltpu.VMEM((depth, wide), BF16),
            pltpu.VMEM(output_weight_matrix.shape, BF16),
            pltpu.VMEM(kv_cache.shape, BF16),
            pltpu.VMEM((N_COL, feats, LANES), F32),
            pltpu.VMEM((depth, 2 * LANES), BF16),
            pltpu.VMEM((QUARTERS, 2, SIDE, block_rows, wide), BF16),
            pltpu.VMEM((QUARTERS, SIDE, block_rows, wide), BF16),
            pltpu.VMEM((QUARTERS, SIDE, block_rows, wide), BF16),
            pltpu.VMEM((QUARTERS, SIDE, block_rows, wide), BF16),
            slabs,
            slabs,
            slabs,
            slabs,
            pltpu.VMEM((N_COL, 16, LANES), F32),
            pltpu.VMEM((N_COL, 16, LANES), F32),
            pltpu.VMEM((2, heads, HD), BF16),
            pltpu.VMEM((ROWS_DEV, 8, kv_cols), F32),
            pltpu.VMEM((QUARTERS, N_ROW, block_rows, head_cols), BF16),
            pltpu.VMEM((CHUNKS, SIDE, SIDE, feats, LANES), BF16),
            pltpu.VMEM((CHUNKS, 2, 2, feats, LANES), BF16),
            pltpu.VMEM((CHUNKS, 2, SIDE, feats, LANES), BF16),
            pltpu.VMEM((CHUNKS, feats, LANES), BF16),
            pltpu.VMEM((CHUNKS, 2, feats, LANES), BF16),
            pltpu.VMEM((CHUNKS, feats, LANES), BF16),
            pltpu.VMEM((SIDE, 24, LANES), F32),
            pltpu.VMEM((SIDE, 48, LANES), F32),
            pltpu.VMEM((SIDE, 16, LANES), F32),
            pltpu.VMEM((2, 16, LANES), F32),
            pltpu.VMEM((24, LANES), F32),
            pltpu.VMEM((48, LANES), F32),
            pltpu.VMEM((16, LANES), F32),
            pltpu.VMEM((16, LANES), F32),
            pltpu.VMEM((16, LANES), F32),
            dma((3,)),
            dma((ROWS_DEV,)),
            dma((QUARTERS, 8)),
            dma((QUARTERS, 8)),
            dma((QUARTERS,)),
            dma((QUARTERS, 4)),
            dma((QUARTERS, 2)),
            dma((QUARTERS, 2)),
            dma((QUARTERS,)),
            dma((QUARTERS,)),
            dma((QUARTERS,)),
            dma((QUARTERS,)),
            dma((4,)),
            dma((4,)),
        ],
        compiler_params=pltpu.CompilerParams(
            collective_id=0, has_side_effects=True, vmem_limit_bytes=VMEM_BYTES
        ),
        name="decode",
    )(
        tokens.T,
        layer_norm_gain,
        query_weight,
        kv_weight,
        output_weight_matrix,
        kv_cache,
        lengths,
    )
    branch, new_kv = hand_over(branch, new_kv)
    return branch.T, new_kv


def solution(mesh):
    placed = (
        P(None, ("row", "col")),
        P(("row", "col")),
        P("row", "col"),
        P("row", None),
        P("col", "row"),
        P(("row", "col"), None, None),
        P(("row", "col")),
    )
    return jax.shard_map(
        shards,
        mesh=mesh,
        in_specs=placed,
        out_specs=(P(None, ("row", "col")), P(("row", "col"), None)),
        check_vma=False,
    )
```

```python
import functools

import jax
import jax.numpy as jnp
from jax import lax
from jax.experimental import pallas as pl
from jax.experimental.pallas import tpu as pltpu
from jax.sharding import PartitionSpec as P

MESH = pl.DeviceIdType.MESH
EPSILON = 1e-05
NEGATIVE_FLOOR = -1e30
HD = 256
SIDE = 4
N_COL = SIDE * SIDE
N_ROW = 8
ROWS_DEV = 8
LANES = 128
GROUPS = ROWS_DEV
CUT, REST = 80, 64
(
    ST_X,
    ST_Z,
    ST_Y,
    ST_C,
    ST_END,
    FIRST,
    FIRST_ON,
    SECOND,
    SECOND_ON,
    PROJECT,
    SUM_CORES,
    ROWS_OUT,
    ATTEND,
    CONTEXTS_OUT,
    CONTEXTS_ON,
    PROJECT_OUT,
    SUM_1B,
    SUM_2A,
    SUM_2B,
    SUM_END,
) = range(20)

ORDER = [
    (FIRST, 3), (FIRST, 7), (FIRST, 0), (ST_X, 0), (FIRST, 5), (FIRST, 1),
    (FIRST, 2), (FIRST, 6), (FIRST_ON, 3), (FIRST_ON, 7), (FIRST_ON, 0), (FIRST, 4),
    (ST_Z, 0), (FIRST_ON, 5), (FIRST_ON, 2), (FIRST_ON, 1), (FIRST_ON, 6), (SECOND, 3),
    (SECOND, 7), (SECOND, 0), (ST_Y, 0), (SECOND_ON, 3), (ST_C, 0), (SECOND, 2),
    (SECOND_ON, 7), (ST_END, 0), (SECOND_ON, 0), (SECOND, 5), (SECOND, 6), (PROJECT, 3),
    (SECOND_ON, 2), (FIRST_ON, 4), (SUM_CORES, 3), (PROJECT, 7), (PROJECT, 0), (SUM_CORES, 7),
    (SECOND_ON, 5), (SUM_CORES, 0), (SECOND, 1), (ROWS_OUT, 3), (SECOND_ON, 6), (PROJECT, 2),
    (SECOND, 4), (PROJECT, 5), (SUM_CORES, 2), (ROWS_OUT, 7), (SECOND_ON, 1), (SUM_CORES, 5),
    (ROWS_OUT, 0), (PROJECT, 6), (ATTEND, 3), (SECOND_ON, 4), (ROWS_OUT, 2), (PROJECT, 1),
    (SUM_CORES, 6), (ATTEND, 7), (ROWS_OUT, 5), (PROJECT, 4), (CONTEXTS_OUT, 3), (SUM_CORES, 1),
    (ATTEND, 0), (SUM_CORES, 4), (ATTEND, 2), (ROWS_OUT, 6), (CONTEXTS_OUT, 7), (ATTEND, 5),
    (CONTEXTS_ON, 3), (ROWS_OUT, 1), (CONTEXTS_OUT, 0), (PROJECT_OUT, 3), (ROWS_OUT, 4), (CONTEXTS_OUT, 2),
    (CONTEXTS_ON, 7), (ATTEND, 6), (PROJECT_OUT, 7), (CONTEXTS_OUT, 5), (CONTEXTS_ON, 0), (SUM_1B, 3),
    (ATTEND, 1), (PROJECT_OUT, 0), (ATTEND, 4), (SUM_1B, 7), (CONTEXTS_ON, 2), (CONTEXTS_OUT, 6),
    (CONTEXTS_ON, 5), (PROJECT_OUT, 2), (PROJECT_OUT, 5), (SUM_1B, 0), (CONTEXTS_OUT, 1), (CONTEXTS_OUT, 4),
    (SUM_2A, 3), (CONTEXTS_ON, 6), (SUM_1B, 2), (PROJECT_OUT, 6), (CONTEXTS_ON, 1), (SUM_1B, 5),
    (CONTEXTS_ON, 4), (PROJECT_OUT, 1), (PROJECT_OUT, 4), (SUM_2A, 7), (SUM_1B, 6), (SUM_1B, 1),
    (SUM_1B, 4), (SUM_2A, 6), (SUM_2A, 5), (SUM_2A, 2), (SUM_2B, 7), (SUM_2A, 0),
    (SUM_2A, 1), (SUM_2A, 4), (SUM_2B, 6), (SUM_2B, 2), (SUM_2B, 3), (SUM_2B, 1),
    (SUM_2B, 0), (SUM_2B, 5), (SUM_2B, 4), (SUM_END, 2), (SUM_END, 6), (SUM_END, 3),
    (SUM_END, 7), (SUM_END, 0), (SUM_END, 1), (SUM_END, 5), (SUM_END, 4),
]
VMEM_BYTES = 60 * 1024 * 1024
F32, BF16 = jnp.float32, jnp.bfloat16


def rcopy(src, dst, send_sem, recv_sem, device):
    return pltpu.make_async_remote_copy(
        src_ref=src,
        dst_ref=dst,
        send_sem=send_sem,
        recv_sem=recv_sem,
        device_id=device,
        device_id_type=MESH,
    )


def along(ax, x, z, step):
    if ax == 0:
        return lax.rem(x + step + SIDE, SIDE) * SIDE + z
    return x * SIDE + lax.rem(z + step + SIDE, SIDE)


def loop(low, high, body):
    def step(i, carry):
        body(i)
        return carry

    lax.fori_loop(low, high, step, 0)


OTHERS = sorted(
    [(i, k) for i in range(SIDE) for k in range(SIDE) if (i, k) != (0, 0)],
    key=lambda at: -min(at[0], SIDE - at[0]) - min(at[1], SIDE - at[1]),
)


def landed(ref, sem):
    pltpu.make_async_copy(ref, ref, sem).wait()


def greet(peers):
    barrier = pltpu.get_barrier_semaphore()
    for peer in peers:
        pl.semaphore_signal(barrier, inc=1, device_id=peer, device_id_type=MESH)


def feats_of(ax, v):
    return (0, CUT) if ax == v else (CUT, REST)


def part_of(ax, v, si):
    low, n = feats_of(ax, v)
    half = (n + 16) // 32 * 16
    return (low, half) if si == 0 else (low + half, n - half)


def by_parity(s, do):
    for v in (0, 1):
        pl.when(lax.rem(s, 2) == v)(lambda v=v: do(v))


def add_into(ref, *terms):
    total = ref[...].astype(F32)
    for term in terms:
        total = total + term[...].astype(F32)
    ref[...] = total.astype(BF16)


def kernel(
    n_features,
    tok,
    gain,
    wq,
    wkv,
    wo,
    cache,
    lengths,
    out,
    kv_out,
    perm,
    xbuf,
    qw,
    ow,
    kvc,
    gexp,
    xn,
    pq,
    pqr,
    yq,
    yqr,
    slab,
    slabr,
    cslab,
    cslabr,
    fold,
    cfold,
    qt,
    kvf,
    allctx,
    pbuf,
    r1a,
    r1b,
    r2a,
    r2b,
    ot,
    stx,
    stz,
    sty,
    stc,
    smsg,
    zmsg,
    ymsg,
    cmsg,
    mi,
    w_sem,
    k_sem,
    gs,
    gr,
    os_,
    or_,
    ps,
    pr,
    as_,
    ar,
    cs,
    cr,
    ss,
    sr,
):
    r, c = lax.axis_index("row"), lax.axis_index("col")
    x, z = lax.div(c, SIDE), lax.rem(c, SIDE)
    y, core = lax.div(r, 2), lax.rem(r, 2)
    partner = r + 1 - 2 * core
    feats = tok.shape[0]
    head_cols = wq.shape[1]
    q_parts = head_cols // LANES
    wide_parts = q_parts + 1
    wide = wide_parts * LANES

    def other(number):
        i, k = OTHERS[number]
        return lax.rem(x + i, SIDE) * SIDE + lax.rem(z + k, SIDE)

    def other_y(d):
        return lax.rem(r + 2 * d + 2, N_ROW)

    peers = [(r, other(d)) for d in range(N_COL - 1)]
    peers += [(other_y(d), c) for d in range(3)] + [(partner, c)]
    greet(peers)

    load_q = pltpu.make_async_copy(wq, qw.at[:, pl.ds(0, head_cols)], w_sem.at[0])
    load_kv = pltpu.make_async_copy(
        wkv.at[:, pl.ds(pl.multiple_of(x * LANES, LANES), LANES)],
        qw.at[:, pl.ds(head_cols, LANES)],
        w_sem.at[1],
    )
    load_o = pltpu.make_async_copy(wo, ow, w_sem.at[2])
    load_q.start()
    load_kv.start()

    def load_cache(b):
        return pltpu.make_async_copy(cache.at[b], kvc.at[b], k_sem.at[b])

    loop(0, ROWS_DEV, lambda b: load_cache(b).start())
    load_o.start()

    row = lax.broadcasted_iota(jnp.int32, (N_ROW * LANES, LANES), 0)
    lane = lax.broadcasted_iota(jnp.int32, (N_ROW * LANES, LANES), 1)
    same = lax.div(row, ROWS_DEV) == lane
    for s in range(GROUPS):
        hit = jnp.logical_and(same, lax.rem(row, ROWS_DEV) == s)
        perm[s] = jnp.where(hit, 1.0, 0.0).astype(BF16)

    sums, squares = [], []
    for s in range(GROUPS):
        t = jnp.dot(tok[...], perm[s], preferred_element_type=F32)
        xbuf[s, x, z] = t.astype(BF16)
        sums.append(jnp.sum(t, axis=0, keepdims=True))
        squares.append(jnp.sum(t * t, axis=0, keepdims=True))
    smsg[0:8] = jnp.concatenate(sums, axis=0)
    smsg[8:16] = jnp.concatenate(squares, axis=0)
    gains = gain[...].astype(F32).reshape(1, feats)
    smsg[16:24] = jnp.zeros((8, LANES), F32)
    smsg[16:17] = gains[:, 0:LANES]
    smsg[17:18, 0 : feats - LANES] = gains[:, LANES:feats]
    stx[x] = smsg[...]

    fold[...] = jnp.zeros_like(fold)
    cfold[...] = jnp.zeros_like(cfold)
    pl.semaphore_wait(pltpu.get_barrier_semaphore(), len(peers))

    def stat_x(d):
        return rcopy(smsg, stx.at[x], ss.at[0], sr.at[0], (r, along(0, x, z, d + 1)))

    def stat_z(d):
        return rcopy(zmsg, stz.at[z], ss.at[1], sr.at[1], (r, along(1, x, z, d + 1)))

    def stat_y(d):
        return rcopy(ymsg, sty.at[y], ss.at[2], sr.at[2], (other_y(d), c))

    stat_c = rcopy(cmsg, stc.at[core], ss.at[3], sr.at[3], (partner, c))

    def mid(ax):
        return x if ax == 0 else z

    def end(ax):
        return z if ax == 0 else x

    def blocks(buf, ax, s, i, low, n, feats):
        i = lax.rem(i + SIDE, SIDE)
        some, f = pl.ds(low, n), pl.ds(*feats)
        return buf.at[s, some, i, f] if ax == 0 else buf.at[s, i, some, f]

    def block(buf, ax, s, i, feats):
        i = lax.rem(i + SIDE, SIDE)
        f = pl.ds(*feats)
        return buf.at[s, i, z, f] if ax == 0 else buf.at[s, x, i, f]

    def first(ax, s, si, v):
        here = block(xbuf, ax, s, mid(ax), feats_of(ax, v))
        return rcopy(here, here, gs.at[0], gr.at[s, 0], (r, along(ax, x, z, 1 - 2 * si)))

    def first_on(ax, s, si, v):
        way = 1 - 2 * si
        ref = block(xbuf, ax, s, mid(ax) - way, part_of(ax, v, si))
        return rcopy(ref, ref, gs.at[1], gr.at[s, 1], (r, along(ax, x, z, way)))

    def second(ax, s, si, v):
        ref = blocks(xbuf, ax, s, end(ax), 0, SIDE, feats_of(ax, v))
        return rcopy(ref, ref, gs.at[2], gr.at[s, 2], (r, along(1 - ax, x, z, 1 - 2 * si)))

    def second_on(ax, s, si, v):
        way = 1 - 2 * si
        ref = blocks(xbuf, ax, s, end(ax) - way, 2 * si, 2, feats_of(ax, v))
        return rcopy(ref, ref, gs.at[3], gr.at[s, 3], (r, along(1 - ax, x, z, way)))

    def ways(s, send):
        def do(v):
            for si in (0, 1):
                for ax in (0, 1):
                    send(ax, s, si, v).start()

        by_parity(s, do)

    def stats_x(s):
        for d in range(3):
            stat_x(d).start()

    def stats_z(s):
        landed(stx.at[pl.ds(0, 3)], sr.at[0])
        zmsg[0:16] = stx[0, 0:16] + stx[1, 0:16] + stx[2, 0:16] + stx[3, 0:16]
        for i in range(SIDE):
            zmsg[16 + 8 * i : 24 + 8 * i] = stx[i, 16:24]
        stz[z] = zmsg[...]
        for d in range(3):
            stat_z(d).start()

    def spread(i):
        rows = stz[i % SIDE, pl.ds(pl.multiple_of(16 + 8 * (i // SIDE), 8), 8)]
        gexp[i, 0:128] = jnp.broadcast_to(rows[0:1], (128, 128)).T
        gexp[i, 128:feats] = jnp.broadcast_to(rows[1:2], (128, 128)).T[0 : feats - 128]

    def stats_y(s):
        landed(stz.at[pl.ds(0, 3)], sr.at[1])
        ymsg[...] = stz[0, 0:16] + stz[1, 0:16] + stz[2, 0:16] + stz[3, 0:16]
        sty[y] = ymsg[...]
        for d in range(3):
            stat_y(d).start()
        loop(0, N_COL, spread)

    def stats_core(s):
        landed(sty.at[pl.ds(0, 3)], sr.at[2])
        cmsg[...] = sty[0] + sty[1] + sty[2] + sty[3]
        stc[core] = cmsg[...]
        stat_c.start()

    def stats_end(s):
        stat_c.wait_recv()
        total = stc[0] + stc[1]
        average = total[0:8] / n_features
        mi[0:8] = average
        mi[8:16] = lax.rsqrt(total[8:16] / n_features - average * average + EPSILON)
        load_q.wait()
        load_kv.wait()
        load_o.wait()

    def tokens_first(s):
        ways(s, first)

    def tokens_first_on(s):
        landed(xbuf.at[s, 0, pl.ds(0, 2)], gr.at[s, 0])
        ways(s, first_on)

    def tokens_second(s):
        landed(xbuf.at[s, 0, 0], gr.at[s, 1])
        ways(s, second)

    def tokens_second_on(s):
        landed(xbuf.at[s, pl.ds(0, 2)], gr.at[s, 2])
        ways(s, second_on)

    def to_partner(s):
        return rcopy(pq.at[s, 1 - core], pqr.at[s], ps.at[0], pr.at[s, 0], (partner, c))

    def project(s):
        landed(xbuf.at[s, 0], gr.at[s, 3])
        mean, inverse = mi[pl.ds(s, 1), :], mi[pl.ds(8 + s, 1), :]
        for i in range(N_COL):
            t = xbuf[s, i // SIDE, i % SIDE].astype(F32)
            xn[feats * i : feats * (i + 1)] = ((t - mean) * inverse * gexp[i]).astype(BF16)
        partial = lax.dot_general(
            xn[...], qw[...], (((0,), (0,)), ((), ())), preferred_element_type=F32
        ).astype(BF16)
        for i in range(N_ROW):
            pq[s, i % 2, i // 2] = partial[N_COL * i : N_COL * (i + 1)]
        to_partner(s).start()

    def to_y(s, d):
        to = other_y(d)
        return rcopy(
            yq.at[s, lax.div(to, 2)], yqr.at[s, y], ps.at[1], pr.at[s, 1], (to, c)
        )

    def sum_cores(s):
        to_partner(s).wait_recv()
        yq[s] = (pq[s, core].astype(F32) + pqr[s].astype(F32)).astype(BF16)
        for d in range(3):
            to_y(s, d).start()
        yqr[s, y] = yq[s, y]

    def scatter(src, dst, send_sem, recv_sem, s, d):
        to = other(d)
        return rcopy(src.at[s, to], dst.at[s, c], send_sem.at[0], recv_sem.at[s], (r, to))

    def rows_out(s):
        landed(yqr.at[s, pl.ds(0, 3)], pr.at[s, 1])
        total = yqr[s, 0].astype(F32)
        for i in range(1, SIDE):
            total = total + yqr[s, i].astype(F32)
        for k in range(wide_parts):
            fold[:, k, :] = total[:, LANES * k : LANES * (k + 1)]
        slab[s] = fold[...].astype(BF16)
        for d in range(N_COL - 1):
            scatter(slab, slabr, as_, ar, s, d).start()
        slabr[s, c] = slab[s, c]

    scale = HD**-0.5

    def attend(s):
        landed(slabr.at[s, pl.ds(0, N_COL - 1)], ar.at[s])
        fold[...] = slabr[s].astype(F32)
        for k in range(q_parts):
            at = slice(N_COL * (k // 2), N_COL * (k // 2 + 1))
            qt[at, LANES * (k % 2) : LANES * (k % 2 + 1)] = fold[:, k, :].astype(BF16)
        for i in range(SIDE):
            kvf[s, 0:1, LANES * i : LANES * (i + 1)] = fold[SIDE * i, q_parts : q_parts + 1, :]
        load_cache(s).wait()
        q = qt[...]
        new_key, new_value = kvf[s, 0:1, :HD], kvf[s, 0:1, HD:]
        position = lax.broadcasted_iota(jnp.int32, (1, kvc.shape[1]), 1)
        scores = (
            lax.dot_general(
                q, kvc[s, :, :HD], (((1,), (1,)), ((), ())), preferred_element_type=F32
            )
            * scale
        )
        scores = jnp.where(position < lengths[s], scores, NEGATIVE_FLOOR)
        new_score = jnp.sum(q.astype(F32) * new_key, axis=1, keepdims=True) * scale
        top = jnp.maximum(jnp.max(scores, axis=1, keepdims=True), new_score)
        weights = jnp.exp(scores - top)
        new_weight = jnp.exp(new_score - top)
        total = jnp.sum(weights, axis=1, keepdims=True) + new_weight
        context = jnp.dot(weights.astype(BF16), kvc[s, :, HD:], preferred_element_type=F32)
        context = context + new_weight.astype(BF16).astype(F32) * new_value
        context = context / total
        for k in range(q_parts):
            cfold[:, k, :] = context[
                N_COL * (k // 2) : N_COL * (k // 2 + 1), LANES * (k % 2) : LANES * (k % 2 + 1)
            ]
        cslab[s] = cfold[...].astype(BF16)
        for d in range(N_COL - 1):
            scatter(cslab, cslabr, cs, cr, s, d).start()
        cslabr[s, c] = cslab[s, c]

    def share(s, d):
        to = (other_y(d), c)
        ref = allctx.at[s, r]
        return rcopy(ref, ref, os_.at[0], or_.at[s, d], to)

    def pass_on(s, d):
        ref = allctx.at[s, lax.rem(r + 2 * (SIDE - 1 - d), N_ROW)]
        return rcopy(ref, ref, os_.at[0], or_.at[s, 3], (partner, c))

    def share_core(s):
        ref = allctx.at[s, r]
        return rcopy(ref, ref, os_.at[0], or_.at[s, 3], (partner, c))

    def contexts_out(s):
        landed(cslabr.at[s, pl.ds(0, N_COL - 1)], cr.at[s])
        cfold[...] = cslabr[s].astype(F32)
        for k in range(q_parts):
            allctx[s, r, :, LANES * k : LANES * (k + 1)] = cfold[:, k, :].astype(BF16)
        for d in range(3):
            share(s, d).start()
        share_core(s).start()

    def contexts_on(s):
        for d in range(3):
            share(s, d).wait_recv()
            pass_on(s, d).start()

    def group(ax, s, i, low, n, feats):
        i = lax.rem(i + SIDE, SIDE)
        some, f = pl.ds(low, n), pl.ds(*feats)
        return pbuf.at[s, i, some, f] if ax == 0 else pbuf.at[s, some, i, f]

    def single(ax, s, i, feats):
        i = lax.rem(i + SIDE, SIDE)
        f = pl.ds(*feats)
        return pbuf.at[s, x, i, f] if ax == 0 else pbuf.at[s, i, z, f]

    def send_1a(ax, s, si, v):
        f = feats_of(ax, v)
        src = group(ax, s, mid(ax) + 2, 2 * si, 2, f)
        to = (r, along(ax, x, z, 1 - 2 * si))
        return rcopy(src, r1a.at[s, si, :, pl.ds(*f)], gs.at[4], gr.at[s, 4], to)

    def send_1b(ax, s, si, v):
        f = feats_of(ax, v)
        src = group(ax, s, mid(ax) + 1 - 2 * si, 0, SIDE, f)
        to = (r, along(ax, x, z, 1 - 2 * si))
        return rcopy(src, r1b.at[s, si, :, pl.ds(*f)], gs.at[5], gr.at[s, 5], to)

    def send_2a(ax, s, si, v):
        f = part_of(ax, v, si)
        src = single(ax, s, end(ax) + 2, f)
        to = (r, along(1 - ax, x, z, 1 - 2 * si))
        return rcopy(src, r2a.at[s, pl.ds(*f)], gs.at[6], gr.at[s, 6], to)

    def send_2b(ax, s, si, v):
        f = feats_of(ax, v)
        src = single(ax, s, end(ax) + 1 - 2 * si, f)
        to = (r, along(1 - ax, x, z, 1 - 2 * si))
        return rcopy(src, r2b.at[s, si, pl.ds(*f)], gs.at[7], gr.at[s, 7], to)

    def project_out(s):
        landed(allctx.at[s, pl.ds(0, 4)], or_.at[s, 3])
        context = allctx[s].reshape(LANES, head_cols)
        term = jnp.dot(context, ow[...], preferred_element_type=F32)
        turned = term.astype(BF16).T
        for i in range(N_COL):
            pbuf[s, i // SIDE, i % SIDE] = turned[feats * i : feats * (i + 1)]
        ways(s, send_1a)

    def sum_1b(s):
        landed(pbuf.at[s, 0], gr.at[s, 4])

        def do(v):
            for ax in (0, 1):
                f = feats_of(ax, v)
                for si in (0, 1):
                    add_into(
                        group(ax, s, mid(ax) + 1 - 2 * si, 2 * si, 2, f),
                        r1a.at[s, si, :, pl.ds(*f)],
                    )
                    send_1b(ax, s, si, v).start()

        by_parity(s, do)

    def sum_2a(s):
        landed(pbuf.at[s, pl.ds(0, 2)], gr.at[s, 5])

        def do(v):
            for ax in (0, 1):
                f = feats_of(ax, v)
                add_into(
                    group(ax, s, mid(ax), 0, SIDE, f),
                    r1b.at[s, 0, :, pl.ds(*f)],
                    r1b.at[s, 1, :, pl.ds(*f)],
                )
                for si in (0, 1):
                    send_2a(ax, s, si, v).start()

        by_parity(s, do)

    def sum_2b(s):
        landed(pbuf.at[s, 0, 0], gr.at[s, 6])

        def do(v):
            for ax in (0, 1):
                for si in (0, 1):
                    f = part_of(ax, v, si)
                    add_into(single(ax, s, end(ax) + 1 - 2 * si, f), r2a.at[s, pl.ds(*f)])
                    send_2b(ax, s, si, v).start()

        by_parity(s, do)

    def sum_end(s):
        landed(pbuf.at[s, 0, pl.ds(0, 2)], gr.at[s, 7])
        total = pbuf[s, x, z].astype(F32) + r2b[s, 0].astype(F32) + r2b[s, 1].astype(F32)
        ot[s] = total.astype(BF16)

    steps = {
        ST_X: stats_x,
        ST_Z: stats_z,
        ST_Y: stats_y,
        ST_C: stats_core,
        ST_END: stats_end,
        FIRST: tokens_first,
        FIRST_ON: tokens_first_on,
        SECOND: tokens_second,
        SECOND_ON: tokens_second_on,
        PROJECT: project,
        SUM_CORES: sum_cores,
        ROWS_OUT: rows_out,
        ATTEND: attend,
        CONTEXTS_OUT: contexts_out,
        CONTEXTS_ON: contexts_on,
        PROJECT_OUT: project_out,
        SUM_1B: sum_1b,
        SUM_2A: sum_2a,
        SUM_2B: sum_2b,
        SUM_END: sum_end,
    }

    def take(step, s, low, high):
        if high - low == 1:
            steps[low](s)
            return
        middle = (low + high) // 2
        pl.when(step < middle)(lambda: take(step, s, low, middle))
        pl.when(step >= middle)(lambda: take(step, s, middle, high))

    base = 256
    codes = [step * GROUPS + s for step, s in ORDER]
    codes += [0] * (-len(codes) % 3)

    def in_order(t):
        at, which = lax.div(t, 3), lax.rem(t, 3)
        word = jnp.int32(0)
        for i in range(0, len(codes), 3):
            number = codes[i] + base * (codes[i + 1] + base * codes[i + 2])
            word = jnp.where(at == i // 3, number, word)
        rest = lax.div(word, base)
        code = jnp.where(which == 0, word, jnp.where(which == 1, rest, lax.div(rest, base)))
        code = lax.rem(code, base)
        take(lax.div(code, GROUPS), lax.rem(code, GROUPS), 0, len(steps))

    loop(0, len(ORDER), in_order)

    total = jnp.zeros(out.shape, F32)
    for s in range(GROUPS):
        total = total + lax.dot_general(
            ot[s], perm[s], (((1,), (1,)), ((), ())), preferred_element_type=F32
        )
    out[...] = total.astype(BF16)
    fresh = [kvf[n, 0:1, :] for n in range(ROWS_DEV)]
    kv_out[...] = jnp.concatenate(fresh, axis=0).astype(BF16)

    landed(stx.at[pl.ds(0, 3)], ss.at[0])
    landed(stz.at[pl.ds(0, 3)], ss.at[1])
    landed(sty.at[pl.ds(0, 3)], ss.at[2])
    stat_c.wait_send()

    landed(xbuf.at[0], gs.at[0])
    landed(xbuf.at[0, pl.ds(0, 2)], gs.at[1])
    landed(xbuf.at[pl.ds(0, 4)], gs.at[2])
    landed(xbuf.at[pl.ds(0, 2)], gs.at[3])
    landed(pbuf.at[pl.ds(0, 2)], gs.at[4])
    landed(pbuf.at[pl.ds(0, 4)], gs.at[5])
    landed(pbuf.at[0, pl.ds(0, 2)], gs.at[6])
    landed(pbuf.at[0], gs.at[7])
    landed(pqr, ps.at[0])
    landed(yqr.at[:, pl.ds(0, 3)], ps.at[1])
    landed(slab.at[:, pl.ds(0, N_COL - 1)], as_.at[0])
    landed(cslab.at[:, pl.ds(0, N_COL - 1)], cs.at[0])
    landed(allctx.at[:, pl.ds(0, 7)], os_.at[0])


def hand_over_kernel(branch, new_kv, branch_out, new_kv_out):
    branch_out[...] = branch[...]
    new_kv_out[...] = new_kv[...]


def hand_over(branch, new_kv):
    vmem = pl.BlockSpec(memory_space=pltpu.VMEM)
    return pl.pallas_call(
        hand_over_kernel,
        out_shape=(
            jax.ShapeDtypeStruct(branch.shape, branch.dtype),
            jax.ShapeDtypeStruct(new_kv.shape, new_kv.dtype),
        ),
        in_specs=[vmem, vmem],
        out_specs=(vmem, vmem),
        name="hand_over",
    )(branch, new_kv)


def shards(
    tokens, layer_norm_gain, query_weight, kv_weight, output_weight_matrix, kv_cache, lengths
):
    devices = lax.axis_size("row") * lax.axis_size("col")
    rows, feats = tokens.shape
    depth, head_cols = query_weight.shape
    heads = head_cols * N_COL // HD
    kv_cols = kv_weight.shape[1]
    wide = head_cols + LANES
    vmem = pl.BlockSpec(memory_space=pltpu.VMEM)
    smem = pl.BlockSpec(memory_space=pltpu.SMEM)
    anywhere = pl.BlockSpec(memory_space=pl.ANY)
    dma = pltpu.SemaphoreType.DMA
    slabs = pltpu.VMEM((GROUPS, N_COL, 8, LANES), BF16)
    branch, new_kv = pl.pallas_call(
        functools.partial(kernel, feats * devices),
        out_shape=(
            jax.ShapeDtypeStruct((feats, rows), BF16),
            jax.ShapeDtypeStruct((ROWS_DEV, kv_cols), BF16),
        ),
        in_specs=[vmem, vmem, anywhere, anywhere, anywhere, anywhere, smem],
        out_specs=(vmem, vmem),
        scratch_shapes=[
            pltpu.VMEM((GROUPS, rows, LANES), BF16),
            pltpu.VMEM((GROUPS, SIDE, SIDE, feats, LANES), BF16),
            pltpu.VMEM((depth, wide), BF16),
            pltpu.VMEM(output_weight_matrix.shape, BF16),
            pltpu.VMEM(kv_cache.shape, BF16),
            pltpu.VMEM((N_COL, feats, LANES), F32),
            pltpu.VMEM((depth, LANES), BF16),
            pltpu.VMEM((GROUPS, 2, SIDE, N_COL, wide), BF16),
            pltpu.VMEM((GROUPS, SIDE, N_COL, wide), BF16),
            pltpu.VMEM((GROUPS, SIDE, N_COL, wide), BF16),
            pltpu.VMEM((GROUPS, SIDE, N_COL, wide), BF16),
            slabs,
            slabs,
            slabs,
            slabs,
            pltpu.VMEM((N_COL, 8, LANES), F32),
            pltpu.VMEM((N_COL, 8, LANES), F32),
            pltpu.VMEM((heads, HD), BF16),
            pltpu.VMEM((ROWS_DEV, 8, kv_cols), F32),
            pltpu.VMEM((GROUPS, N_ROW, N_COL, head_cols), BF16),
            pltpu.VMEM((GROUPS, SIDE, SIDE, feats, LANES), BF16),
            pltpu.VMEM((GROUPS, 2, 2, feats, LANES), BF16),
            pltpu.VMEM((GROUPS, 2, SIDE, feats, LANES), BF16),
            pltpu.VMEM((GROUPS, feats, LANES), BF16),
            pltpu.VMEM((GROUPS, 2, feats, LANES), BF16),
            pltpu.VMEM((GROUPS, feats, LANES), BF16),
            pltpu.VMEM((SIDE, 24, LANES), F32),
            pltpu.VMEM((SIDE, 48, LANES), F32),
            pltpu.VMEM((SIDE, 16, LANES), F32),
            pltpu.VMEM((2, 16, LANES), F32),
            pltpu.VMEM((24, LANES), F32),
            pltpu.VMEM((48, LANES), F32),
            pltpu.VMEM((16, LANES), F32),
            pltpu.VMEM((16, LANES), F32),
            pltpu.VMEM((16, LANES), F32),
            dma((3,)),
            dma((ROWS_DEV,)),
            dma((8,)),
            dma((GROUPS, 8)),
            dma((1,)),
            dma((GROUPS, 4)),
            dma((2,)),
            dma((GROUPS, 2)),
            dma((1,)),
            dma((GROUPS,)),
            dma((1,)),
            dma((GROUPS,)),
            dma((4,)),
            dma((4,)),
        ],
        compiler_params=pltpu.CompilerParams(
            collective_id=0, has_side_effects=True, vmem_limit_bytes=VMEM_BYTES
        ),
        name="decode",
    )(
        tokens.T,
        layer_norm_gain,
        query_weight,
        kv_weight,
        output_weight_matrix,
        kv_cache,
        lengths,
    )
    branch, new_kv = hand_over(branch, new_kv)
    return branch.T, new_kv


def solution(mesh):
    placed = (
        P(None, ("row", "col")),
        P(("row", "col")),
        P("row", "col"),
        P("row", None),
        P("col", "row"),
        P(("row", "col"), None, None),
        P(("row", "col")),
    )
    return jax.shard_map(
        shards,
        mesh=mesh,
        in_specs=placed,
        out_specs=(P(None, ("row", "col")), P(("row", "col"), None)),
        check_vma=False,
    )
```

```python
import functools

import jax
import jax.numpy as jnp
from jax import lax
from jax.experimental import pallas as pl
from jax.experimental.pallas import tpu as pltpu
from jax.sharding import PartitionSpec as P

MESH = pl.DeviceIdType.MESH
EPSILON = 1e-05
NEGATIVE_FLOOR = -1e30
HD = 256
SIDE = 4
N_COL = SIDE * SIDE
N_ROW = 8
ROWS_DEV = 8
LANES = 128
GROUPS = ROWS_DEV
CUT, REST = 80, 64
(
    ST_X,
    ST_Z,
    ST_Y,
    ST_C,
    ST_END,
    FIRST,
    FIRST_ON,
    SECOND,
    SECOND_ON,
    PROJECT,
    SUM_CORES,
    ROWS_OUT,
    ATTEND,
    CONTEXTS_OUT,
    CONTEXTS_ON,
    PROJECT_OUT,
    SUM_1B,
    SUM_2A,
    SUM_2B,
    SUM_END,
) = range(20)

ORDER = [
    (FIRST, 1), (ST_X, 0), (FIRST, 5), (FIRST, 6), (FIRST, 2), (FIRST, 3),
    (FIRST, 7), (FIRST, 4), (FIRST_ON, 1), (ST_Z, 0), (FIRST, 0), (FIRST_ON, 6),
    (FIRST_ON, 2), (FIRST_ON, 3), (FIRST_ON, 7), (FIRST_ON, 5), (FIRST_ON, 4), (SECOND, 1),
    (SECOND, 2), (SECOND, 3), (ST_Y, 0), (SECOND_ON, 1), (SECOND, 4), (ST_C, 0),
    (SECOND_ON, 2), (ST_END, 0), (SECOND_ON, 3), (SECOND, 5), (PROJECT, 1), (SUM_CORES, 1),
    (SECOND_ON, 4), (FIRST_ON, 0), (SECOND, 7), (PROJECT, 2), (PROJECT, 3), (SUM_CORES, 2),
    (SECOND_ON, 5), (SECOND, 6), (SUM_CORES, 3), (PROJECT, 4), (ROWS_OUT, 1), (SUM_CORES, 4),
    (SECOND_ON, 7), (SECOND, 0), (PROJECT, 5), (ROWS_OUT, 2), (SECOND_ON, 6), (ROWS_OUT, 3),
    (SUM_CORES, 5), (PROJECT, 7), (ATTEND, 1), (ROWS_OUT, 4), (SECOND_ON, 0), (PROJECT, 6),
    (SUM_CORES, 7), (ATTEND, 2), (SUM_CORES, 6), (ATTEND, 3), (CONTEXTS_OUT, 1), (ROWS_OUT, 5),
    (PROJECT, 0), (ATTEND, 4), (SUM_CORES, 0), (ROWS_OUT, 7), (CONTEXTS_OUT, 2), (CONTEXTS_ON, 1),
    (ROWS_OUT, 6), (CONTEXTS_OUT, 3), (PROJECT_OUT, 1), (ATTEND, 5), (ROWS_OUT, 0), (CONTEXTS_OUT, 4),
    (ATTEND, 7), (SUM_1B, 1), (CONTEXTS_ON, 2), (CONTEXTS_ON, 3), (ATTEND, 6), (PROJECT_OUT, 3),
    (CONTEXTS_OUT, 5), (PROJECT_OUT, 2), (CONTEXTS_ON, 4), (ATTEND, 0), (PROJECT_OUT, 4), (CONTEXTS_OUT, 7),
    (SUM_1B, 3), (CONTEXTS_OUT, 6), (SUM_1B, 2), (CONTEXTS_ON, 5), (PROJECT_OUT, 5), (SUM_1B, 4),
    (CONTEXTS_OUT, 0), (CONTEXTS_ON, 7), (CONTEXTS_ON, 6), (PROJECT_OUT, 7), (PROJECT_OUT, 6), (SUM_1B, 5),
    (CONTEXTS_ON, 0), (PROJECT_OUT, 0), (SUM_2A, 4), (SUM_1B, 7), (SUM_1B, 6), (SUM_1B, 0),
    (SUM_2A, 7), (SUM_2A, 5), (SUM_2B, 4), (SUM_2A, 1), (SUM_2A, 2), (SUM_2A, 6),
    (SUM_2A, 3), (SUM_2A, 0), (SUM_2B, 7), (SUM_2B, 5), (SUM_2B, 1), (SUM_2B, 6),
    (SUM_2B, 3), (SUM_2B, 2), (SUM_2B, 0), (SUM_END, 5), (SUM_END, 3), (SUM_END, 7),
    (SUM_END, 1), (SUM_END, 6), (SUM_END, 4), (SUM_END, 2), (SUM_END, 0),
]
VMEM_BYTES = 60 * 1024 * 1024
F32, BF16 = jnp.float32, jnp.bfloat16


def rcopy(src, dst, send_sem, recv_sem, device):
    return pltpu.make_async_remote_copy(
        src_ref=src,
        dst_ref=dst,
        send_sem=send_sem,
        recv_sem=recv_sem,
        device_id=device,
        device_id_type=MESH,
    )


def along(ax, x, z, step):
    if ax == 0:
        return lax.rem(x + step + SIDE, SIDE) * SIDE + z
    return x * SIDE + lax.rem(z + step + SIDE, SIDE)


def loop(low, high, body):
    def step(i, carry):
        body(i)
        return carry

    lax.fori_loop(low, high, step, 0)


OTHERS = sorted(
    [(i, k) for i in range(SIDE) for k in range(SIDE) if (i, k) != (0, 0)],
    key=lambda at: -min(at[0], SIDE - at[0]) - min(at[1], SIDE - at[1]),
)


def landed(ref, sem):
    pltpu.make_async_copy(ref, ref, sem).wait()


def greet(peers):
    barrier = pltpu.get_barrier_semaphore()
    for peer in peers:
        pl.semaphore_signal(barrier, inc=1, device_id=peer, device_id_type=MESH)


def feats_of(ax, v):
    return (0, CUT) if ax == v else (CUT, REST)


def part_of(ax, v, si):
    low, n = feats_of(ax, v)
    half = (n + 16) // 32 * 16
    return (low, half) if si == 0 else (low + half, n - half)


def by_parity(s, do):
    for v in (0, 1):
        pl.when(lax.rem(s, 2) == v)(lambda v=v: do(v))


def add_into(ref, *terms):
    total = ref[...].astype(F32)
    for term in terms:
        total = total + term[...].astype(F32)
    ref[...] = total.astype(BF16)


def kernel(
    n_features,
    tok,
    gain,
    wq,
    wkv,
    wo,
    cache,
    lengths,
    out,
    kv_out,
    perm,
    xbuf,
    qw,
    ow,
    kvc,
    gexp,
    xn,
    pq,
    pqr,
    yq,
    yqr,
    slab,
    slabr,
    cslab,
    cslabr,
    fold,
    cfold,
    qt,
    kvf,
    allctx,
    pbuf,
    r1a,
    r1b,
    r2a,
    r2b,
    ot,
    stx,
    stz,
    sty,
    stc,
    smsg,
    zmsg,
    ymsg,
    cmsg,
    mi,
    w_sem,
    k_sem,
    gs,
    gr,
    os_,
    or_,
    ps,
    pr,
    as_,
    ar,
    cs,
    cr,
    ss,
    sr,
):
    r, c = lax.axis_index("row"), lax.axis_index("col")
    x, z = lax.div(c, SIDE), lax.rem(c, SIDE)
    y, core = lax.div(r, 2), lax.rem(r, 2)
    partner = r + 1 - 2 * core
    feats = tok.shape[0]
    head_cols = wq.shape[1]
    q_parts = head_cols // LANES
    wide_parts = q_parts + 1
    wide = wide_parts * LANES

    def other(number):
        i, k = OTHERS[number]
        return lax.rem(x + i, SIDE) * SIDE + lax.rem(z + k, SIDE)

    def other_y(d):
        return lax.rem(r + 2 * d + 2, N_ROW)

    peers = [(r, other(d)) for d in range(N_COL - 1)]
    peers += [(other_y(d), c) for d in range(3)] + [(partner, c)]
    greet(peers)

    load_q = pltpu.make_async_copy(wq, qw.at[:, pl.ds(0, head_cols)], w_sem.at[0])
    load_kv = pltpu.make_async_copy(
        wkv.at[:, pl.ds(pl.multiple_of(x * LANES, LANES), LANES)],
        qw.at[:, pl.ds(head_cols, LANES)],
        w_sem.at[1],
    )
    load_o = pltpu.make_async_copy(wo, ow, w_sem.at[2])
    load_q.start()
    load_kv.start()

    def load_cache(b):
        return pltpu.make_async_copy(cache.at[b], kvc.at[b], k_sem.at[b])

    loop(0, ROWS_DEV, lambda b: load_cache(b).start())
    load_o.start()

    row = lax.broadcasted_iota(jnp.int32, (N_ROW * LANES, LANES), 0)
    lane = lax.broadcasted_iota(jnp.int32, (N_ROW * LANES, LANES), 1)
    same = lax.div(row, ROWS_DEV) == lane
    for s in range(GROUPS):
        hit = jnp.logical_and(same, lax.rem(row, ROWS_DEV) == s)
        perm[s] = jnp.where(hit, 1.0, 0.0).astype(BF16)

    sums, squares = [], []
    for s in range(GROUPS):
        t = jnp.dot(tok[...], perm[s], preferred_element_type=F32)
        xbuf[s, x, z] = t.astype(BF16)
        sums.append(jnp.sum(t, axis=0, keepdims=True))
        squares.append(jnp.sum(t * t, axis=0, keepdims=True))
    smsg[0:8] = jnp.concatenate(sums, axis=0)
    smsg[8:16] = jnp.concatenate(squares, axis=0)
    gains = gain[...].astype(F32).reshape(1, feats)
    smsg[16:24] = jnp.zeros((8, LANES), F32)
    smsg[16:17] = gains[:, 0:LANES]
    smsg[17:18, 0 : feats - LANES] = gains[:, LANES:feats]
    stx[x] = smsg[...]

    fold[...] = jnp.zeros_like(fold)
    cfold[...] = jnp.zeros_like(cfold)
    pl.semaphore_wait(pltpu.get_barrier_semaphore(), len(peers))

    def stat_x(d):
        return rcopy(smsg, stx.at[x], ss.at[0], sr.at[0], (r, along(0, x, z, d + 1)))

    def stat_z(d):
        return rcopy(zmsg, stz.at[z], ss.at[1], sr.at[1], (r, along(1, x, z, d + 1)))

    def stat_y(d):
        return rcopy(ymsg, sty.at[y], ss.at[2], sr.at[2], (other_y(d), c))

    stat_c = rcopy(cmsg, stc.at[core], ss.at[3], sr.at[3], (partner, c))

    def mid(ax):
        return x if ax == 0 else z

    def end(ax):
        return z if ax == 0 else x

    def blocks(buf, ax, s, i, low, n, feats):
        i = lax.rem(i + SIDE, SIDE)
        some, f = pl.ds(low, n), pl.ds(*feats)
        return buf.at[s, some, i, f] if ax == 0 else buf.at[s, i, some, f]

    def block(buf, ax, s, i, feats):
        i = lax.rem(i + SIDE, SIDE)
        f = pl.ds(*feats)
        return buf.at[s, i, z, f] if ax == 0 else buf.at[s, x, i, f]

    def first(ax, s, si, v):
        here = block(xbuf, ax, s, mid(ax), feats_of(ax, v))
        return rcopy(here, here, gs.at[0], gr.at[s, 0], (r, along(ax, x, z, 1 - 2 * si)))

    def first_on(ax, s, si, v):
        way = 1 - 2 * si
        ref = block(xbuf, ax, s, mid(ax) - way, part_of(ax, v, si))
        return rcopy(ref, ref, gs.at[1], gr.at[s, 1], (r, along(ax, x, z, way)))

    def second(ax, s, si, v):
        ref = blocks(xbuf, ax, s, end(ax), 0, SIDE, feats_of(ax, v))
        return rcopy(ref, ref, gs.at[2], gr.at[s, 2], (r, along(1 - ax, x, z, 1 - 2 * si)))

    def second_on(ax, s, si, v):
        way = 1 - 2 * si
        ref = blocks(xbuf, ax, s, end(ax) - way, 2 * si, 2, feats_of(ax, v))
        return rcopy(ref, ref, gs.at[3], gr.at[s, 3], (r, along(1 - ax, x, z, way)))

    def ways(s, send):
        def do(v):
            for si in (0, 1):
                for ax in (0, 1):
                    send(ax, s, si, v).start()

        by_parity(s, do)

    def stats_x(s):
        for d in range(3):
            stat_x(d).start()

    def stats_z(s):
        landed(stx.at[pl.ds(0, 3)], sr.at[0])
        zmsg[0:16] = stx[0, 0:16] + stx[1, 0:16] + stx[2, 0:16] + stx[3, 0:16]
        for i in range(SIDE):
            zmsg[16 + 8 * i : 24 + 8 * i] = stx[i, 16:24]
        stz[z] = zmsg[...]
        for d in range(3):
            stat_z(d).start()

    def spread(i):
        rows = stz[i % SIDE, pl.ds(pl.multiple_of(16 + 8 * (i // SIDE), 8), 8)]
        gexp[i, 0:128] = jnp.broadcast_to(rows[0:1], (128, 128)).T
        gexp[i, 128:feats] = jnp.broadcast_to(rows[1:2], (128, 128)).T[0 : feats - 128]

    def stats_y(s):
        landed(stz.at[pl.ds(0, 3)], sr.at[1])
        ymsg[...] = stz[0, 0:16] + stz[1, 0:16] + stz[2, 0:16] + stz[3, 0:16]
        sty[y] = ymsg[...]
        for d in range(3):
            stat_y(d).start()
        loop(0, N_COL, spread)

    def stats_core(s):
        landed(sty.at[pl.ds(0, 3)], sr.at[2])
        cmsg[...] = sty[0] + sty[1] + sty[2] + sty[3]
        stc[core] = cmsg[...]
        stat_c.start()

    def stats_end(s):
        stat_c.wait_recv()
        total = stc[0] + stc[1]
        average = total[0:8] / n_features
        mi[0:8] = average
        mi[8:16] = lax.rsqrt(total[8:16] / n_features - average * average + EPSILON)
        load_q.wait()
        load_kv.wait()
        load_o.wait()

    def tokens_first(s):
        ways(s, first)

    def tokens_first_on(s):
        landed(xbuf.at[s, 0, pl.ds(0, 2)], gr.at[s, 0])
        ways(s, first_on)

    def tokens_second(s):
        landed(xbuf.at[s, 0, 0], gr.at[s, 1])
        ways(s, second)

    def tokens_second_on(s):
        landed(xbuf.at[s, pl.ds(0, 2)], gr.at[s, 2])
        ways(s, second_on)

    def to_partner(s):
        return rcopy(pq.at[s, 1 - core], pqr.at[s], ps.at[0], pr.at[s, 0], (partner, c))

    def project(s):
        landed(xbuf.at[s, 0], gr.at[s, 3])
        mean, inverse = mi[pl.ds(s, 1), :], mi[pl.ds(8 + s, 1), :]
        for i in range(N_COL):
            t = xbuf[s, i // SIDE, i % SIDE].astype(F32)
            xn[feats * i : feats * (i + 1)] = ((t - mean) * inverse * gexp[i]).astype(BF16)
        partial = lax.dot_general(
            xn[...], qw[...], (((0,), (0,)), ((), ())), preferred_element_type=F32
        ).astype(BF16)
        for i in range(N_ROW):
            pq[s, i % 2, i // 2] = partial[N_COL * i : N_COL * (i + 1)]
        to_partner(s).start()

    def to_y(s, d):
        to = other_y(d)
        return rcopy(
            yq.at[s, lax.div(to, 2)], yqr.at[s, y], ps.at[1], pr.at[s, 1], (to, c)
        )

    def sum_cores(s):
        to_partner(s).wait_recv()
        yq[s] = (pq[s, core].astype(F32) + pqr[s].astype(F32)).astype(BF16)
        for d in range(3):
            to_y(s, d).start()
        yqr[s, y] = yq[s, y]

    def scatter(src, dst, send_sem, recv_sem, s, d):
        to = other(d)
        return rcopy(src.at[s, to], dst.at[s, c], send_sem.at[0], recv_sem.at[s], (r, to))

    def rows_out(s):
        landed(yqr.at[s, pl.ds(0, 3)], pr.at[s, 1])
        total = yqr[s, 0].astype(F32)
        for i in range(1, SIDE):
            total = total + yqr[s, i].astype(F32)
        for k in range(wide_parts):
            fold[:, k, :] = total[:, LANES * k : LANES * (k + 1)]
        slab[s] = fold[...].astype(BF16)
        for d in range(N_COL - 1):
            scatter(slab, slabr, as_, ar, s, d).start()
        slabr[s, c] = slab[s, c]

    scale = HD**-0.5

    def attend(s):
        landed(slabr.at[s, pl.ds(0, N_COL - 1)], ar.at[s])
        fold[...] = slabr[s].astype(F32)
        for k in range(q_parts):
            at = slice(N_COL * (k // 2), N_COL * (k // 2 + 1))
            qt[at, LANES * (k % 2) : LANES * (k % 2 + 1)] = fold[:, k, :].astype(BF16)
        for i in range(SIDE):
            kvf[s, 0:1, LANES * i : LANES * (i + 1)] = fold[SIDE * i, q_parts : q_parts + 1, :]
        load_cache(s).wait()
        q = qt[...]
        new_key, new_value = kvf[s, 0:1, :HD], kvf[s, 0:1, HD:]
        position = lax.broadcasted_iota(jnp.int32, (1, kvc.shape[1]), 1)
        scores = (
            lax.dot_general(
                q, kvc[s, :, :HD], (((1,), (1,)), ((), ())), preferred_element_type=F32
            )
            * scale
        )
        scores = jnp.where(position < lengths[s], scores, NEGATIVE_FLOOR)
        new_score = jnp.sum(q.astype(F32) * new_key, axis=1, keepdims=True) * scale
        top = jnp.maximum(jnp.max(scores, axis=1, keepdims=True), new_score)
        weights = jnp.exp(scores - top)
        new_weight = jnp.exp(new_score - top)
        total = jnp.sum(weights, axis=1, keepdims=True) + new_weight
        context = jnp.dot(weights.astype(BF16), kvc[s, :, HD:], preferred_element_type=F32)
        context = context + new_weight.astype(BF16).astype(F32) * new_value
        context = context / total
        for k in range(q_parts):
            cfold[:, k, :] = context[
                N_COL * (k // 2) : N_COL * (k // 2 + 1), LANES * (k % 2) : LANES * (k % 2 + 1)
            ]
        cslab[s] = cfold[...].astype(BF16)
        for d in range(N_COL - 1):
            scatter(cslab, cslabr, cs, cr, s, d).start()
        cslabr[s, c] = cslab[s, c]

    def share(s, d):
        to = (other_y(d), c)
        ref = allctx.at[s, r]
        return rcopy(ref, ref, os_.at[0], or_.at[s, d], to)

    def pass_on(s, d):
        ref = allctx.at[s, lax.rem(r + 2 * (SIDE - 1 - d), N_ROW)]
        return rcopy(ref, ref, os_.at[0], or_.at[s, 3], (partner, c))

    def share_core(s):
        ref = allctx.at[s, r]
        return rcopy(ref, ref, os_.at[0], or_.at[s, 3], (partner, c))

    def contexts_out(s):
        landed(cslabr.at[s, pl.ds(0, N_COL - 1)], cr.at[s])
        cfold[...] = cslabr[s].astype(F32)
        for k in range(q_parts):
            allctx[s, r, :, LANES * k : LANES * (k + 1)] = cfold[:, k, :].astype(BF16)
        for d in range(3):
            share(s, d).start()
        share_core(s).start()

    def contexts_on(s):
        for d in range(3):
            share(s, d).wait_recv()
            pass_on(s, d).start()

    def group(ax, s, i, low, n, feats):
        i = lax.rem(i + SIDE, SIDE)
        some, f = pl.ds(low, n), pl.ds(*feats)
        return pbuf.at[s, i, some, f] if ax == 0 else pbuf.at[s, some, i, f]

    def single(ax, s, i, feats):
        i = lax.rem(i + SIDE, SIDE)
        f = pl.ds(*feats)
        return pbuf.at[s, x, i, f] if ax == 0 else pbuf.at[s, i, z, f]

    def send_1a(ax, s, si, v):
        f = feats_of(ax, v)
        src = group(ax, s, mid(ax) + 2, 2 * si, 2, f)
        to = (r, along(ax, x, z, 1 - 2 * si))
        return rcopy(src, r1a.at[s, si, :, pl.ds(*f)], gs.at[4], gr.at[s, 4], to)

    def send_1b(ax, s, si, v):
        f = feats_of(ax, v)
        src = group(ax, s, mid(ax) + 1 - 2 * si, 0, SIDE, f)
        to = (r, along(ax, x, z, 1 - 2 * si))
        return rcopy(src, r1b.at[s, si, :, pl.ds(*f)], gs.at[5], gr.at[s, 5], to)

    def send_2a(ax, s, si, v):
        f = part_of(ax, v, si)
        src = single(ax, s, end(ax) + 2, f)
        to = (r, along(1 - ax, x, z, 1 - 2 * si))
        return rcopy(src, r2a.at[s, pl.ds(*f)], gs.at[6], gr.at[s, 6], to)

    def send_2b(ax, s, si, v):
        f = feats_of(ax, v)
        src = single(ax, s, end(ax) + 1 - 2 * si, f)
        to = (r, along(1 - ax, x, z, 1 - 2 * si))
        return rcopy(src, r2b.at[s, si, pl.ds(*f)], gs.at[7], gr.at[s, 7], to)

    def project_out(s):
        landed(allctx.at[s, pl.ds(0, 4)], or_.at[s, 3])
        context = allctx[s].reshape(LANES, head_cols)
        term = jnp.dot(context, ow[...], preferred_element_type=F32)
        turned = term.astype(BF16).T
        for i in range(N_COL):
            pbuf[s, i // SIDE, i % SIDE] = turned[feats * i : feats * (i + 1)]
        ways(s, send_1a)

    def sum_1b(s):
        landed(pbuf.at[s, 0], gr.at[s, 4])

        def do(v):
            for ax in (0, 1):
                f = feats_of(ax, v)
                for si in (0, 1):
                    add_into(
                        group(ax, s, mid(ax) + 1 - 2 * si, 2 * si, 2, f),
                        r1a.at[s, si, :, pl.ds(*f)],
                    )
                    send_1b(ax, s, si, v).start()

        by_parity(s, do)

    def sum_2a(s):
        landed(pbuf.at[s, pl.ds(0, 2)], gr.at[s, 5])

        def do(v):
            for ax in (0, 1):
                f = feats_of(ax, v)
                add_into(
                    group(ax, s, mid(ax), 0, SIDE, f),
                    r1b.at[s, 0, :, pl.ds(*f)],
                    r1b.at[s, 1, :, pl.ds(*f)],
                )
                for si in (0, 1):
                    send_2a(ax, s, si, v).start()

        by_parity(s, do)

    def sum_2b(s):
        landed(pbuf.at[s, 0, 0], gr.at[s, 6])

        def do(v):
            for ax in (0, 1):
                for si in (0, 1):
                    f = part_of(ax, v, si)
                    add_into(single(ax, s, end(ax) + 1 - 2 * si, f), r2a.at[s, pl.ds(*f)])
                    send_2b(ax, s, si, v).start()

        by_parity(s, do)

    def sum_end(s):
        landed(pbuf.at[s, 0, pl.ds(0, 2)], gr.at[s, 7])
        total = pbuf[s, x, z].astype(F32) + r2b[s, 0].astype(F32) + r2b[s, 1].astype(F32)
        ot[s] = total.astype(BF16)

    steps = {
        ST_X: stats_x,
        ST_Z: stats_z,
        ST_Y: stats_y,
        ST_C: stats_core,
        ST_END: stats_end,
        FIRST: tokens_first,
        FIRST_ON: tokens_first_on,
        SECOND: tokens_second,
        SECOND_ON: tokens_second_on,
        PROJECT: project,
        SUM_CORES: sum_cores,
        ROWS_OUT: rows_out,
        ATTEND: attend,
        CONTEXTS_OUT: contexts_out,
        CONTEXTS_ON: contexts_on,
        PROJECT_OUT: project_out,
        SUM_1B: sum_1b,
        SUM_2A: sum_2a,
        SUM_2B: sum_2b,
        SUM_END: sum_end,
    }

    def take(step, s, low, high):
        if high - low == 1:
            steps[low](s)
            return
        middle = (low + high) // 2
        pl.when(step < middle)(lambda: take(step, s, low, middle))
        pl.when(step >= middle)(lambda: take(step, s, middle, high))

    base = 256
    codes = [step * GROUPS + s for step, s in ORDER]
    codes += [0] * (-len(codes) % 3)

    def in_order(t):
        at, which = lax.div(t, 3), lax.rem(t, 3)
        word = jnp.int32(0)
        for i in range(0, len(codes), 3):
            number = codes[i] + base * (codes[i + 1] + base * codes[i + 2])
            word = jnp.where(at == i // 3, number, word)
        rest = lax.div(word, base)
        code = jnp.where(which == 0, word, jnp.where(which == 1, rest, lax.div(rest, base)))
        code = lax.rem(code, base)
        take(lax.div(code, GROUPS), lax.rem(code, GROUPS), 0, len(steps))

    loop(0, len(ORDER), in_order)

    total = jnp.zeros(out.shape, F32)
    for s in range(GROUPS):
        total = total + lax.dot_general(
            ot[s], perm[s], (((1,), (1,)), ((), ())), preferred_element_type=F32
        )
    out[...] = total.astype(BF16)
    fresh = [kvf[n, 0:1, :] for n in range(ROWS_DEV)]
    kv_out[...] = jnp.concatenate(fresh, axis=0).astype(BF16)

    landed(stx.at[pl.ds(0, 3)], ss.at[0])
    landed(stz.at[pl.ds(0, 3)], ss.at[1])
    landed(sty.at[pl.ds(0, 3)], ss.at[2])
    stat_c.wait_send()

    landed(xbuf.at[0], gs.at[0])
    landed(xbuf.at[0, pl.ds(0, 2)], gs.at[1])
    landed(xbuf.at[pl.ds(0, 4)], gs.at[2])
    landed(xbuf.at[pl.ds(0, 2)], gs.at[3])
    landed(pbuf.at[pl.ds(0, 2)], gs.at[4])
    landed(pbuf.at[pl.ds(0, 4)], gs.at[5])
    landed(pbuf.at[0, pl.ds(0, 2)], gs.at[6])
    landed(pbuf.at[0], gs.at[7])
    landed(pqr, ps.at[0])
    landed(yqr.at[:, pl.ds(0, 3)], ps.at[1])
    landed(slab.at[:, pl.ds(0, N_COL - 1)], as_.at[0])
    landed(cslab.at[:, pl.ds(0, N_COL - 1)], cs.at[0])
    landed(allctx.at[:, pl.ds(0, 7)], os_.at[0])


def hand_over_kernel(branch, new_kv, branch_out, new_kv_out):
    branch_out[...] = branch[...]
    new_kv_out[...] = new_kv[...]


def hand_over(branch, new_kv):
    vmem = pl.BlockSpec(memory_space=pltpu.VMEM)
    return pl.pallas_call(
        hand_over_kernel,
        out_shape=(
            jax.ShapeDtypeStruct(branch.shape, branch.dtype),
            jax.ShapeDtypeStruct(new_kv.shape, new_kv.dtype),
        ),
        in_specs=[vmem, vmem],
        out_specs=(vmem, vmem),
        name="hand_over",
    )(branch, new_kv)


def shards(
    tokens, layer_norm_gain, query_weight, kv_weight, output_weight_matrix, kv_cache, lengths
):
    devices = lax.axis_size("row") * lax.axis_size("col")
    rows, feats = tokens.shape
    depth, head_cols = query_weight.shape
    heads = head_cols * N_COL // HD
    kv_cols = kv_weight.shape[1]
    wide = head_cols + LANES
    vmem = pl.BlockSpec(memory_space=pltpu.VMEM)
    smem = pl.BlockSpec(memory_space=pltpu.SMEM)
    anywhere = pl.BlockSpec(memory_space=pl.ANY)
    dma = pltpu.SemaphoreType.DMA
    slabs = pltpu.VMEM((GROUPS, N_COL, 8, LANES), BF16)
    branch, new_kv = pl.pallas_call(
        functools.partial(kernel, feats * devices),
        out_shape=(
            jax.ShapeDtypeStruct((feats, rows), BF16),
            jax.ShapeDtypeStruct((ROWS_DEV, kv_cols), BF16),
        ),
        in_specs=[vmem, vmem, anywhere, anywhere, anywhere, anywhere, smem],
        out_specs=(vmem, vmem),
        scratch_shapes=[
            pltpu.VMEM((GROUPS, rows, LANES), BF16),
            pltpu.VMEM((GROUPS, SIDE, SIDE, feats, LANES), BF16),
            pltpu.VMEM((depth, wide), BF16),
            pltpu.VMEM(output_weight_matrix.shape, BF16),
            pltpu.VMEM(kv_cache.shape, BF16),
            pltpu.VMEM((N_COL, feats, LANES), F32),
            pltpu.VMEM((depth, LANES), BF16),
            pltpu.VMEM((GROUPS, 2, SIDE, N_COL, wide), BF16),
            pltpu.VMEM((GROUPS, SIDE, N_COL, wide), BF16),
            pltpu.VMEM((GROUPS, SIDE, N_COL, wide), BF16),
            pltpu.VMEM((GROUPS, SIDE, N_COL, wide), BF16),
            slabs,
            slabs,
            slabs,
            slabs,
            pltpu.VMEM((N_COL, 8, LANES), F32),
            pltpu.VMEM((N_COL, 8, LANES), F32),
            pltpu.VMEM((heads, HD), BF16),
            pltpu.VMEM((ROWS_DEV, 8, kv_cols), F32),
            pltpu.VMEM((GROUPS, N_ROW, N_COL, head_cols), BF16),
            pltpu.VMEM((GROUPS, SIDE, SIDE, feats, LANES), BF16),
            pltpu.VMEM((GROUPS, 2, 2, feats, LANES), BF16),
            pltpu.VMEM((GROUPS, 2, SIDE, feats, LANES), BF16),
            pltpu.VMEM((GROUPS, feats, LANES), BF16),
            pltpu.VMEM((GROUPS, 2, feats, LANES), BF16),
            pltpu.VMEM((GROUPS, feats, LANES), BF16),
            pltpu.VMEM((SIDE, 24, LANES), F32),
            pltpu.VMEM((SIDE, 48, LANES), F32),
            pltpu.VMEM((SIDE, 16, LANES), F32),
            pltpu.VMEM((2, 16, LANES), F32),
            pltpu.VMEM((24, LANES), F32),
            pltpu.VMEM((48, LANES), F32),
            pltpu.VMEM((16, LANES), F32),
            pltpu.VMEM((16, LANES), F32),
            pltpu.VMEM((16, LANES), F32),
            dma((3,)),
            dma((ROWS_DEV,)),
            dma((8,)),
            dma((GROUPS, 8)),
            dma((1,)),
            dma((GROUPS, 4)),
            dma((2,)),
            dma((GROUPS, 2)),
            dma((1,)),
            dma((GROUPS,)),
            dma((1,)),
            dma((GROUPS,)),
            dma((4,)),
            dma((4,)),
        ],
        compiler_params=pltpu.CompilerParams(
            collective_id=0, has_side_effects=True, vmem_limit_bytes=VMEM_BYTES
        ),
        name="decode",
    )(
        tokens.T,
        layer_norm_gain,
        query_weight,
        kv_weight,
        output_weight_matrix,
        kv_cache,
        lengths,
    )
    branch, new_kv = hand_over(branch, new_kv)
    return branch.T, new_kv


def solution(mesh):
    placed = (
        P(None, ("row", "col")),
        P(("row", "col")),
        P("row", "col"),
        P("row", None),
        P("col", "row"),
        P(("row", "col"), None, None),
        P(("row", "col")),
    )
    return jax.shard_map(
        shards,
        mesh=mesh,
        in_specs=placed,
        out_specs=(P(None, ("row", "col")), P(("row", "col"), None)),
        check_vma=False,
    )
```
